32 devices in a mesh: groups: 2 (over x), dom: 16 (over z, y, core).
Axes of the slice: x: 2, y: 2, z: 4, core: 2. Of those that a mesh axis runs over, the one named last changes fastest.
Arguments:
- particle_places: float32 [16, 3, 3072], P('groups', None, 'dom'), parts along dimension 0, may hold values from 0 to 48, as said below
- particle_speeds: float32 [16, 3, 3072], P('groups', None, 'dom'), parts along dimension 0, may hold values from -7 to 7
- thermal_targets: float32 [16], P('groups'), parts along dimension 0, may hold values from 0.5 to 2
- element_features: bfloat16 [6144, 128], P(('groups', 'dom')), parts along dimension 0, may hold values from -4 to 4
- swap_counterpart_slot: int32 [16], P('groups'), parts along dimension 0, may hold values from 0 to 7, as said below
- swap_approval_flags: int32 [16], P('groups'), parts along dimension 0, may hold values from 0 to 1, as said below
- initial_signal_projector: bfloat16 [128, 128], replicated, may hold values from -0.5 to 0.5
- initial_distance_filter: float32 [8, 128], replicated, may hold values from -2 to 2
- initial_directional_scales: float32 [128], replicated, may hold values from 0.5 to 1.5
- invariant_revision_matrix: bfloat16 [128, 128], replicated, may hold values from -0.5 to 0.5
- magnitude_revision_matrix: bfloat16 [128, 128], replicated, may hold values from -0.5 to 0.5
- later_signal_projector: bfloat16 [128, 128], replicated, may hold values from -0.5 to 0.5
- later_directional_scales: float32 [128], replicated, may hold values from 0.5 to 1.5
- push_output_matrix: float32 [128], replicated, may hold values from -0.5 to 0.5
Outputs:
- positions_new: float32 [16, 3, 3072], P('groups', None, 'dom'), parts along dimension 0
- velocities_new: float32 [16, 3, 3072], P('groups', None, 'dom'), parts along dimension 0
- forces_new: float32 [16, 3, 3072], P('groups', None, 'dom'), parts along dimension 0
The draws below stay inside these ranges and needn't reach their ends.
There are 2 independent parts, one for each index of `groups`. The reference program is written for one: setup_inputs(seed, part) draws one part's arguments, and reference() takes and returns one part's arrays. A program takes and returns all parts, laid end to end along the dimension named above; an argument that names none is the same for every part. Nothing has to cross between parts.
Inputs may be any that keep to these rules, and one draw needn't show every extreme that they name: `particle_places`: the atoms of cell k have x and y in [0, 1) and z in [k, k + 1). `swap_counterpart_slot`: an involution that pairs neighbouring replicas, either (0, 1), (2, 3), ... or (1, 2), (3, 4), ..., a replica left without a pair being its own partner. `swap_approval_flags`: equal for the two replicas of a pair, 0 for a replica that is its own partner.
All inputs are finite; a program needn't handle non-finite values.
Results may differ from the reference program's by a relative error of at most 0.012.
The reference program's roundings to bfloat16 on the way count: a program that leaves them out, or rounds other values in their place, can miss the bound.
Values may be sent and summed in bfloat16 or wider, within the bound.
No kernel may reach another device: no remote copies, remote signals or barrier semaphores. Data moves between devices by JAX's collectives and lax.ppermute only.
A program may use at most 64 MiB of HBM per device.

```python
import math
import jax
import jax.numpy as jnp
from jax import lax

LADDER_RUNGS = 8
NA = 64
HC = 1
F = 128
K = 8
STEPS = 4
NC = 48
ATOMS = 3072


def draw_particle_places(key, part):
    spread = jax.random.uniform(jax.random.fold_in(key, 3), (LADDER_RUNGS, 3, ATOMS), jnp.float32)
    cell_rows = (jnp.arange(ATOMS) // NA).astype(jnp.float32)
    lifted = jnp.array([0.0, 0.0, 1.0], jnp.float32)[None, :, None] * cell_rows[None, None, :]
    return spread + lifted


def draw_particle_speeds(key, part):
    cell_frac = (jnp.arange(ATOMS) // NA).astype(jnp.float32) / NC
    drawn_base = jnp.clip(jax.random.normal(jax.random.fold_in(key, 5), (LADDER_RUNGS, 3, ATOMS), jnp.float32), -4.0, 4.0)
    return drawn_base * jnp.sqrt(1.0 + 2.0 * cell_frac)[None, None, :]


def swap_table(key, part):
    coin_parity = jax.random.randint(jax.random.fold_in(key, 7), (), 0, 2)
    parity = (coin_parity + jnp.asarray(part, jnp.int32)) % 2
    ladder_slot = jnp.arange(LADDER_RUNGS)
    paired = ladder_slot + 1 - 2 * ((ladder_slot + parity) % 2)
    exchange_mate = jnp.where((paired < 0) | (paired >= LADDER_RUNGS), ladder_slot, paired)
    coin_flips = jax.random.randint(jax.random.fold_in(key, 11), (LADDER_RUNGS,), 0, 2)
    coin_flips = jnp.where(ladder_slot == parity, 1, coin_flips)
    coin_flips = jnp.where(ladder_slot == LADDER_RUNGS - 2 - parity, 0, coin_flips)
    low_index = jnp.minimum(ladder_slot, exchange_mate)
    accepted = coin_flips[low_index]
    accepted = jnp.where(exchange_mate == ladder_slot, 0, accepted)
    return (exchange_mate.astype(jnp.int32), accepted.astype(jnp.int32))


def draw_swap_counterpart_slot(key, part):
    return swap_table(key, part)[0]


def draw_swap_approval_flags(key, part):
    return swap_table(key, part)[1]


def shard_levels(own_key, extent, cuts, least, largest):
    def one(position, blocks):
        draws = jax.random.uniform(jax.random.fold_in(jax.random.fold_in(own_key, 6), position), (blocks,), jnp.float32, least / len(cuts), largest / len(cuts))
        return jnp.repeat(jnp.exp(draws), extent[position] // blocks).reshape((-1,) + (1,) * (len(extent) - position - 1))

    factor_of = one(*cuts[0])
    for cut in cuts[1:]:
        factor_of = factor_of * one(*cut)
    return factor_of


def bell_draw(own_key, dims, width, reach, pieces=(), kind=jnp.bfloat16):
    values = jax.random.normal(own_key, dims, jnp.float32) * width
    if len(pieces) > 0:
        values = shard_levels(own_key, dims, pieces, -0.22, 0.18) * values
    return jnp.clip(values, min=-reach, max=reach).astype(kind)


def setup_inputs(seed: int = 0, part: int = 0) -> dict:
    key_of = jax.random.split(jax.random.key(seed), 15)
    part_splits = jax.random.split(jax.random.fold_in(key_of[14], part), 15)
    particle_places = draw_particle_places(jax.random.fold_in(jax.random.fold_in(key_of[14], part), 71), part)
    particle_speeds = draw_particle_speeds(jax.random.fold_in(jax.random.fold_in(key_of[14], part), 71), part)
    thermal_targets = jnp.clip(jnp.exp(jax.random.uniform(part_splits[2], (LADDER_RUNGS,), jnp.float32, math.log(0.5), math.log(2.0))), 0.5, 2.0)
    element_features = bell_draw(part_splits[3], (ATOMS, F), 1.0, 4.0, ((0, 16),))
    swap_counterpart_slot = draw_swap_counterpart_slot(jax.random.fold_in(jax.random.fold_in(key_of[14], part), 71), part)
    swap_approval_flags = draw_swap_approval_flags(jax.random.fold_in(jax.random.fold_in(key_of[14], part), 71), part)
    initial_signal_projector = bell_draw(key_of[6], (F, F), F ** -0.5, 0.5)
    initial_distance_filter = bell_draw(key_of[7], (K, F), K ** -0.5, 2.0, (), jnp.float32)
    initial_directional_scales = jnp.clip(jax.random.uniform(key_of[8], (F,), jnp.float32, 0.5, 1.5), 0.5, 1.5)
    invariant_revision_matrix = bell_draw(key_of[9], (F, F), F ** -0.5, 0.5)
    magnitude_revision_matrix = bell_draw(key_of[10], (F, F), F ** -0.5, 0.5)
    later_signal_projector = bell_draw(key_of[11], (F, F), F ** -0.5, 0.5)
    later_directional_scales = jnp.clip(jax.random.uniform(key_of[12], (F,), jnp.float32, 0.5, 1.5), 0.5, 1.5)
    push_output_matrix = bell_draw(key_of[13], (F,), F ** -0.5, 0.5, (), jnp.float32)
    return dict(particle_places=particle_places, particle_speeds=particle_speeds, thermal_targets=thermal_targets, element_features=element_features, swap_counterpart_slot=swap_counterpart_slot, swap_approval_flags=swap_approval_flags, initial_signal_projector=initial_signal_projector, initial_distance_filter=initial_distance_filter, initial_directional_scales=initial_directional_scales, invariant_revision_matrix=invariant_revision_matrix, magnitude_revision_matrix=magnitude_revision_matrix, later_signal_projector=later_signal_projector, later_directional_scales=later_directional_scales, push_output_matrix=push_output_matrix)


step_time = 0.05
motion_work_lower_limit = 1e-06

def radial_rows(own_coords, part_coords, basis_count):
    displacement = part_coords[:, :, :, None, :] - own_coords[:, :, :, :, None]
    squared = lax.optimization_barrier(jnp.sum(displacement * displacement, axis=1))
    envelope = jnp.where(squared < 1.0, (1.0 - squared) * (1.0 - squared), 0.0)
    vectors = jnp.moveaxis(displacement * envelope[:, None], 1, 3)
    if basis_count == 0:
        return vectors.astype(jnp.bfloat16)
    centers = jnp.arange(basis_count, dtype=jnp.float32) / (basis_count - 1)
    sharpness = 2.0 * (basis_count - 1) * (basis_count - 1)
    offset = squared[:, :, :, None, :] - centers[:, None]
    gaussians = jnp.exp(-sharpness * offset * offset) * envelope[:, :, :, None, :]
    return jnp.concatenate([gaussians, vectors], axis=3).astype(jnp.bfloat16)

def periodic_pad(source_array, width_atoms, along_axis):
    length = source_array.shape[along_axis]
    head_part = lax.slice_in_dim(source_array, length - width_atoms, length, axis=along_axis)
    tail_part = lax.slice_in_dim(source_array, 0, width_atoms, axis=along_axis)
    return jnp.concatenate([head_part, source_array, tail_part], axis=along_axis)

def force_field(location_triples, element_features, first_table, initial_distance_filter, initial_directional_scales, invariant_revision_matrix, magnitude_revision_matrix, later_signal_projector, later_directional_scales, push_output_matrix):
    replicas = location_triples.shape[0]
    cell_total = location_triples.shape[2] // NA
    channels = invariant_revision_matrix.shape[0]
    basis_count = initial_distance_filter.shape[0]
    reach_atoms = (2 * HC + 1) * NA
    padded = periodic_pad(location_triples, HC * NA, 2)
    cell_number = jnp.arange(padded.shape[2], dtype=jnp.int32) // NA - HC
    wrap_shift = (jnp.where(cell_number < 0, -1.0, 0.0) + jnp.where(cell_number >= cell_total, 1.0, 0.0)) * cell_total
    axis_mask = jnp.array([0.0, 0.0, 1.0], jnp.float32)
    near_coords = padded + axis_mask[None, :, None] * wrap_shift[None, None, :]

    def windows(cell_index):
        own_coords = lax.dynamic_slice_in_dim(near_coords, (cell_index + HC) * NA, NA, 2)
        part_coords = lax.dynamic_slice_in_dim(near_coords, cell_index * NA, reach_atoms, 2)
        return (own_coords[:, :, None], part_coords[:, :, None])

    def layer_one(cell_index):
        own_coords, part_coords = windows(cell_index)
        single_row_count = lax.optimization_barrier(radial_rows(own_coords, part_coords, basis_count)).astype(jnp.float32)
        exchange_mate = lax.dynamic_slice_in_dim(first_table, cell_index * NA, reach_atoms, 0).astype(jnp.float32)
        reduced_sum = jnp.einsum('rcaxb,bf->rcaxf', single_row_count, exchange_mate, precision=lax.Precision.HIGHEST)[:, 0]
        scalar = lax.optimization_barrier(jnp.sum(reduced_sum[:, :, :basis_count] * initial_distance_filter, axis=2))
        vector_one = reduced_sum[:, :, basis_count:] * initial_directional_scales
        norm_square = lax.optimization_barrier(jnp.sum(vector_one * vector_one, axis=2))
        update = jnp.dot(scalar.astype(jnp.bfloat16).reshape(-1, channels), invariant_revision_matrix, preferred_element_type=jnp.float32)
        update = update + jnp.dot(norm_square.astype(jnp.bfloat16).reshape(-1, channels), magnitude_revision_matrix, preferred_element_type=jnp.float32)
        self_rows = lax.dynamic_slice_in_dim(element_features, cell_index * NA, NA, 0).astype(jnp.float32)
        hidden = (self_rows[None] + jax.nn.silu(update).reshape(replicas, NA, channels)).astype(jnp.bfloat16)
        return (hidden, vector_one)
    cell_list = jnp.arange(cell_total, dtype=jnp.int32)
    hidden_all, vector_all = lax.map(layer_one, cell_list)
    hidden_rows = jnp.moveaxis(hidden_all, 0, 1).reshape(replicas * cell_total * NA, channels)
    second = jnp.dot(hidden_rows, later_signal_projector, preferred_element_type=jnp.float32).astype(jnp.bfloat16)
    second_table = periodic_pad(second.reshape(replicas, cell_total * NA, channels), HC * NA, 1)

    def layer_two(cell_index):
        own_coords, part_coords = windows(cell_index)
        rows_two = lax.optimization_barrier(radial_rows(own_coords, part_coords, 0)).astype(jnp.float32)
        exchange_mate = lax.dynamic_slice_in_dim(second_table, cell_index * NA, reach_atoms, 1).astype(jnp.float32)
        reduced_sum = jnp.einsum('rcaxb,rbf->rcaxf', rows_two, exchange_mate, precision=lax.Precision.HIGHEST)[:, 0]
        total = vector_all[cell_index] + reduced_sum * later_directional_scales
        return lax.optimization_barrier(jnp.sum(total * push_output_matrix, axis=3))
    force_cells = lax.map(layer_two, cell_list)
    return jnp.transpose(force_cells, (1, 3, 0, 2)).reshape(replicas, 3, cell_total * NA)

def reference(particle_places, particle_speeds, thermal_targets, element_features, swap_counterpart_slot, swap_approval_flags, initial_signal_projector, initial_distance_filter, initial_directional_scales, invariant_revision_matrix, magnitude_revision_matrix, later_signal_projector, later_directional_scales, push_output_matrix):
    particle_number_overall = particle_places.shape[2]
    first_table = periodic_pad(jnp.dot(element_features, initial_signal_projector, preferred_element_type=jnp.float32).astype(jnp.bfloat16), HC * NA, 0)

    def evaluate(location_triples):
        return force_field(location_triples, element_features, first_table, initial_distance_filter, initial_directional_scales, invariant_revision_matrix, magnitude_revision_matrix, later_signal_projector, later_directional_scales, push_output_matrix)
    location_triples = particle_places
    speed_entry = particle_speeds
    present_push = evaluate(location_triples)
    for step_index in range(STEPS):
        half_velocity = speed_entry + 0.5 * step_time * present_push
        location_triples = location_triples + step_time * half_velocity
        present_push = evaluate(location_triples)
        speed_entry = half_velocity + 0.5 * step_time * present_push
        motion_work_amount = lax.optimization_barrier(jnp.sum(speed_entry * speed_entry, axis=(1, 2)))
        stretch_multiplier = jnp.sqrt(thermal_targets / (motion_work_amount / (3.0 * particle_number_overall) + motion_work_lower_limit))
        speed_entry = speed_entry * stretch_multiplier[:, None, None]
    ladder_slot = jnp.arange(thermal_targets.shape[0], dtype=jnp.int32)
    source = jnp.where(swap_approval_flags > 0, swap_counterpart_slot, ladder_slot)
    selected_entries = (source[:, None] == ladder_slot[None, :]).astype(jnp.float32)

    def select_entries(values):
        return lax.optimization_barrier(jnp.sum(selected_entries[:, :, None, None] * values[None], axis=1))
    thermal_ratio = jnp.sqrt(thermal_targets / lax.optimization_barrier(jnp.sum(selected_entries * thermal_targets[None, :], axis=1)))
    atom_cell = (jnp.arange(particle_number_overall, dtype=jnp.int32) // NA).astype(jnp.float32)
    cell_floor = jnp.array([0.0, 0.0, 1.0], jnp.float32)[:, None] * atom_cell[None, :]
    return (select_entries(location_triples) - cell_floor[None], select_entries(speed_entry) * thermal_ratio[:, None, None], select_entries(present_push))
```

```python
import functools
import math

import jax
import jax.numpy as jnp
from jax import lax
from jax.experimental import pallas as pl
from jax.experimental.pallas import tpu as pltpu
from jax.sharding import PartitionSpec as P

NA = 64
PAIR = 2 * NA
STEPS = 4

step_time = 0.05
motion_work_lower_limit = 1e-06
LOG2E = math.log2(math.e)


def dot(a, b):
    return jnp.dot(a, b, preferred_element_type=jnp.float32)


def dot_rows(a, b):
    return lax.dot_general(a, b, (((1,), (1,)), ((), ())), preferred_element_type=jnp.float32)


def pieces(value, count):
    width = value.shape[1]
    row = lax.broadcasted_iota(jnp.int32, (16, width), 0)
    tile = jnp.zeros((16, width), jnp.float32)
    for index in range(count):
        part = value.astype(jnp.bfloat16).astype(jnp.float32)
        tile = jnp.where(row == index, part, tile)
        value = value - part
    return tile.astype(jnp.bfloat16)


def swap_halves(first, second):
    low = lax.broadcasted_iota(jnp.int32, first.shape, first.ndim - 1) < NA
    return pltpu.roll(jnp.where(low, second, first), NA, first.ndim - 1)


def basis(displacement, basis_count):
    dx, dy, dz = displacement
    rest = jnp.maximum(1.0 - (dx * dx + dy * dy + dz * dz), 0.0)
    envelope = rest * rest
    vectors = [dx * envelope, dy * envelope, dz * envelope]
    span = basis_count - 1
    rate = 2.0 * span * LOG2E
    offset = 0.5 - rest
    center = jnp.exp2((-2.0 * span * span * LOG2E) * (offset * offset)) * envelope
    slope = rate * offset
    up = jnp.exp2(slope)
    down = jnp.exp2(-slope)
    up_two = up * up
    down_two = down * down
    rising = [center * up]
    falling = [center * down]
    for _ in range(basis_count // 2 - 1):
        rising.append(rising[-1] * up_two)
        falling.append(falling[-1] * down_two)
    return falling[::-1] + rising, vectors


def simulate(
    thermal_ref,
    x_ref,
    v_ref,
    feat_ref,
    first_ref,
    filter_ref,
    scale_one_ref,
    mix_ref,
    later_ref,
    scale_two_ref,
    push_ref,
    x_out,
    v_out,
    g_out,
    table,
    h_rows,
    e_rows,
    radial_0,
    radial_1,
    vec_rows,
    w_rows,
    u_rows,
    f_rows,
    v_rows,
    g_rows,
):
    atoms = x_ref.shape[1]
    pairs = atoms // PAIR
    cells = float(atoms // NA)
    basis_count = filter_ref.shape[0]
    channels = filter_ref.shape[1]
    lane = lax.broadcasted_iota(jnp.int32, (1, PAIR), 1)
    low = lane < NA
    sub = lax.broadcasted_iota(jnp.int32, (8, PAIR), 0)
    z_only = (sub == 2).astype(jnp.float32)

    def make_table(q, _):
        rows = dot(feat_ref[pl.ds(q * PAIR, PAIR), :], first_ref[...]).astype(jnp.bfloat16)
        table[pl.ds(NA + q * PAIR, PAIR), :] = rows
        return 0

    lax.fori_loop(0, pairs, make_table, 0, unroll=2)
    table[0:NA, :] = table[atoms : atoms + NA, :]
    table[atoms + NA : atoms + PAIR, :] = table[NA:PAIR, :]
    push = push_ref[...]
    push_one = pieces(push * scale_one_ref[...], 2)
    push_two = pieces(
        jnp.sum(dot_rows(pieces(push * scale_two_ref[...], 3), later_ref[...]), axis=0, keepdims=True), 2
    )

    def make_w(q, _):
        w = dot_rows(push_one, table[pl.ds(NA + q * PAIR, PAIR), :])
        w_rows[q] = jnp.broadcast_to(w[0:1] + w[1:2], (8, PAIR))
        return 0

    lax.fori_loop(0, pairs, make_w, 0, unroll=2)
    span = basis_count - 1
    order = lax.broadcasted_iota(jnp.int32, (basis_count, 1), 0).astype(jnp.float32) - 0.5 * span
    filters = filter_ref[...] * jnp.exp(-2.0 * order * order)
    scale_square = scale_one_ref[...] * scale_one_ref[...]

    zero_rows = jnp.zeros((5, PAIR), jnp.float32)

    def load(q, _):
        at = pl.ds(q * PAIR, PAIR)
        h_rows[q + 1] = jnp.concatenate([x_ref[:, at], zero_rows], axis=0)
        v_rows[q] = jnp.concatenate([v_ref[:, at], zero_rows], axis=0)
        return 0

    for q in range(pairs):
        at = slice(q * PAIR, (q + 1) * PAIR)
        h_rows[q + 1] = jnp.concatenate([x_ref[:, at], zero_rows], axis=0)
        v_rows[q] = jnp.concatenate([v_ref[:, at], zero_rows], axis=0)
    g_rows[...] = jnp.zeros(g_rows.shape, jnp.float32)

    def make_rows(q, radial):
        columns = jnp.transpose(h_rows[q + 1])
        before = e_rows[q]
        after = e_rows[q + 1]
        across = jnp.where(low, after, before)
        for chunk in range(NA // 16):
            start = chunk * 16
            own_a = [columns[start : start + 16, c : c + 1] for c in range(3)]
            own_b = [columns[NA + start : NA + start + 16, c : c + 1] for c in range(3)]
            own_a = [jnp.broadcast_to(o, (16, PAIR)) for o in own_a]
            own_b = [jnp.broadcast_to(o, (16, PAIR)) for o in own_b]
            blocks = (
                ([before[c : c + 1] - own_a[c] for c in range(3)], ((0, 0),)),
                ([across[c : c + 1] - jnp.where(low, own_a[c], own_b[c]) for c in range(3)], ((0, 1), (1, 0))),
                ([after[c : c + 1] - own_b[c] for c in range(3)], ((1, 1),)),
            )
            for displacement, places in blocks:
                radials, vectors = basis(displacement, basis_count)
                for index, value in enumerate(radials):
                    value = value.astype(jnp.bfloat16)
                    for own, half in places:
                        radial[
                            own, index * NA + start : index * NA + start + 16, half * PAIR : (half + 1) * PAIR
                        ] = value
                for c, value in enumerate(vectors):
                    value = value.astype(jnp.bfloat16)
                    for own, half in places:
                        at = c * PAIR + own * NA + start
                        vec_rows[q, at : at + 16, half * PAIR : (half + 1) * PAIR] = value

    blank = jnp.zeros((NA, channels), jnp.bfloat16)

    def use_rows(q, radial):
        near = table[pl.ds(pl.multiple_of(q * PAIR, PAIR), 2 * PAIR), :]
        signals = (
            jnp.concatenate([near[: 3 * NA], blank], axis=0),
            jnp.concatenate([blank, near[NA:]], axis=0),
        )
        scalars, norms = [], []
        for own in range(2):
            vectors = jnp.concatenate(
                [vec_rows[q, c * PAIR + own * NA : c * PAIR + own * NA + NA, :] for c in range(3)], axis=0
            )
            vectors = dot(vectors, signals[own])
            norm = vectors[:NA] * vectors[:NA]
            for c in range(1, 3):
                part = vectors[c * NA : (c + 1) * NA]
                norm = norm + part * part
            norms.append((norm * scale_square).astype(jnp.bfloat16))
            sums = dot(radial[own], signals[own])
            scalar = sums[:NA] * filters[0:1]
            for k in range(1, basis_count):
                scalar = scalar + sums[k * NA : (k + 1) * NA] * filters[k : k + 1]
            scalars.append(scalar.astype(jnp.bfloat16))
        messages = jnp.concatenate(
            [jnp.concatenate(scalars, axis=0), jnp.concatenate(norms, axis=0)], axis=1
        )
        half = 0.5 * dot(messages, mix_ref[...])
        own_features = feat_ref[pl.ds(pl.multiple_of(q * PAIR, PAIR), PAIR), :].astype(jnp.float32)
        hidden = (own_features + (half + half * jnp.tanh(half))).astype(jnp.bfloat16)
        u = dot_rows(push_two, hidden)
        u_rows[q + 1] = jnp.broadcast_to(u[0:1] + u[1:2], (8, PAIR)) + w_rows[q]

    row16 = lax.broadcasted_iota(jnp.int32, (16, 2 * PAIR), 0)

    def make_force(q, _):
        before = swap_halves(u_rows[q], u_rows[q + 1])
        after = swap_halves(u_rows[q + 1], u_rows[q + 2])
        first = jnp.concatenate([before, jnp.where(low, after, 0.0)], axis=1)
        second = jnp.concatenate([jnp.where(low, 0.0, before), after], axis=1)
        first = jnp.concatenate([first, first], axis=0)
        second = jnp.concatenate([second, second], axis=0)
        value = jnp.where(row16 < 8, first, second)
        high = value.astype(jnp.bfloat16).astype(jnp.float32)
        value = jnp.where((row16 & 7) == 0, high, jnp.where((row16 & 7) == 1, value - high, 0.0))
        sums = dot_rows(value.astype(jnp.bfloat16), vec_rows[q])
        tile = jnp.zeros((8, PAIR), jnp.float32)
        for c in range(3):
            part = sums[:, c * PAIR : (c + 1) * PAIR]
            part = jnp.sum(jnp.where(low, part[:8], part[8:]), axis=0, keepdims=True)
            tile = jnp.where(sub == c, part, tile)
        f_rows[q] = tile
        return 0

    def step(n, _):
        dt = jnp.where(n == 0, 0.0, step_time).astype(jnp.float32)
        h = v_rows[...] + (0.5 * dt) * g_rows[...]
        v_rows[...] = h
        h_rows[1 : pairs + 1] = h_rows[1 : pairs + 1] + dt * h
        h_rows[0] = h_rows[pairs] - cells * z_only
        h_rows[pairs + 1] = h_rows[1] + cells * z_only

        def shift(q, _):
            e_rows[q] = swap_halves(h_rows[q], h_rows[q + 1])
            return 0

        lax.fori_loop(0, pairs + 1, shift, 0)
        make_rows(0, radial_0)

        def two(i, _):
            q = 2 * i
            use_rows(q, radial_0)
            make_rows(q + 1, radial_1)
            use_rows(q + 1, radial_1)
            make_rows(jnp.minimum(q + 2, pairs - 1), radial_0)
            return 0

        lax.fori_loop(0, pairs // 2, two, 0)
        u_rows[0] = u_rows[pairs]
        u_rows[pairs + 1] = u_rows[1]
        lax.fori_loop(0, pairs, make_force, 0, unroll=2)
        g = f_rows[...]
        g_rows[...] = g
        v = v_rows[...] + (0.5 * dt) * g
        kinetic = jnp.sum(v * v, axis=0)
        kinetic = jnp.sum(jnp.sum(kinetic, axis=1, keepdims=True), axis=0, keepdims=True)
        stretch = jnp.sqrt(thermal_ref[0, 0] / (kinetic / (3.0 * atoms) + motion_work_lower_limit))
        stretch = jnp.where(n == 0, 1.0, stretch)
        v_rows[...] = v * stretch
        return 0

    lax.fori_loop(0, STEPS + 1, step, 0)
    for q in range(pairs):
        at = slice(q * PAIR, (q + 1) * PAIR)
        x_out[:, at] = h_rows[q + 1, 0:3, :]
        v_out[:, at] = v_rows[q, 0:3, :]
        g_out[:, at] = g_rows[q, 0:3, :]


def run_replica(thermal, x, v, features, weights):
    atoms = x.shape[1]
    channels = features.shape[1]
    pairs = atoms // PAIR
    basis_count = weights[1].shape[0]
    out = jax.ShapeDtypeStruct((3, atoms), jnp.float32)
    vmem = pl.BlockSpec(memory_space=pltpu.VMEM)
    tiles = pltpu.VMEM((pairs, 8, PAIR), jnp.float32)
    tiles_two = pltpu.VMEM((pairs + 2, 8, PAIR), jnp.float32)
    radial = pltpu.VMEM((2, basis_count * NA, 2 * PAIR), jnp.bfloat16)
    return pl.pallas_call(
        simulate,
        out_shape=(out, out, out),
        in_specs=[pl.BlockSpec(memory_space=pltpu.SMEM)] + [vmem] * 10,
        out_specs=(vmem, vmem, vmem),
        scratch_shapes=[
            pltpu.VMEM((atoms + PAIR, channels), jnp.bfloat16),
            tiles_two,
            tiles_two,
            radial,
            radial,
            pltpu.VMEM((pairs, 3 * PAIR, 2 * PAIR), jnp.bfloat16),
            tiles,
            tiles_two,
            tiles,
            tiles,
            tiles,
        ],
        compiler_params=pltpu.CompilerParams(vmem_limit_bytes=50 * 1024 * 1024),
    )(thermal, x, v, features, *weights)


def on_device(
    particle_places,
    particle_speeds,
    thermal_targets,
    element_features,
    swap_counterpart_slot,
    swap_approval_flags,
    initial_signal_projector,
    initial_distance_filter,
    initial_directional_scales,
    invariant_revision_matrix,
    magnitude_revision_matrix,
    later_signal_projector,
    later_directional_scales,
    push_output_matrix,
):
    replicas = particle_places.shape[0]
    local_atoms = particle_places.shape[2]
    local_cells = local_atoms // NA
    devices = lax.axis_size("dom")
    own = lax.axis_index("dom")
    per_replica = devices // replicas
    bits = devices.bit_length() - 1
    replica_bits = replicas.bit_length() - 1

    def trade(value, mask):
        return lax.ppermute(value, "dom", [(i, i ^ mask) for i in range(devices)])

    state = jnp.concatenate([particle_places, particle_speeds], axis=1)
    features = element_features
    for level in range(bits):
        mask = devices >> (level + 1)
        upper = (own & mask) > 0
        if level < replica_bits:
            half = state.shape[0] // 2
            keep = jnp.where(upper, state[half:], state[:half])
            send = jnp.where(upper, state[:half], state[half:])
        else:
            keep = send = state
        got = trade(send, mask)
        got_features = trade(features, mask)
        axis = 1 + level
        state = jnp.stack([jnp.where(upper, got, keep), jnp.where(upper, keep, got)], axis=axis)
        features = jnp.stack(
            [jnp.where(upper, got_features, features), jnp.where(upper, features, got_features)], axis=level
        )
        if level + 1 < bits:
            state, features = lax.optimization_barrier((state, features))
    state = state.reshape(devices, 6, local_atoms).transpose(1, 0, 2).reshape(6, devices * local_atoms)
    features = features.reshape(devices * local_atoms, -1)
    thermal = lax.dynamic_slice(thermal_targets, (own // per_replica,), (1,)).reshape(1, 1)
    weights = (
        initial_signal_projector,
        initial_distance_filter,
        initial_directional_scales[None],
        jnp.concatenate([invariant_revision_matrix, magnitude_revision_matrix], axis=0),
        later_signal_projector,
        later_directional_scales[None],
        push_output_matrix[None],
    )
    x, v, g = run_replica(thermal, state[:3], state[3:], features, weights)

    state = jnp.concatenate([x, v, g], axis=0).reshape(9, replicas, per_replica, local_atoms)
    state = lax.dynamic_index_in_dim(state, own % per_replica, 2, keepdims=False)
    state = state.transpose(1, 0, 2)[:, None]
    for level in range(replica_bits):
        mask = devices >> (level + 1)
        upper = (own & mask) > 0
        half = state.shape[0] // 2
        keep = jnp.where(upper, state[half:], state[:half])
        send = jnp.where(upper, state[:half], state[half:])
        got = trade(send, mask)
        state = jnp.stack([jnp.where(upper, got, keep), jnp.where(upper, keep, got)], axis=1 + level)
    state = state.reshape(replicas, 3, 3, local_atoms)

    ladder_slot = jnp.arange(replicas, dtype=jnp.int32)
    source = jnp.where(swap_approval_flags > 0, swap_counterpart_slot, ladder_slot)
    chosen = source[:, None] == ladder_slot[None, :]
    state = jnp.sum(jnp.where(chosen[:, :, None, None, None], state[None], 0.0), axis=1)
    thermal_source = jnp.sum(jnp.where(chosen, thermal_targets[None, :], 0.0), axis=1)
    thermal_ratio = jnp.sqrt(thermal_targets / thermal_source)
    atom_cell = (own * local_cells + jnp.arange(local_atoms, dtype=jnp.int32) // NA).astype(jnp.float32)
    cell_floor = jnp.array([0.0, 0.0, 1.0], jnp.float32)[:, None] * atom_cell[None, :]
    return (
        state[:, 0] - cell_floor[None],
        state[:, 1] * thermal_ratio[:, None, None],
        state[:, 2],
    )


def solution(mesh):
    return jax.shard_map(
        on_device,
        mesh=mesh,
        in_specs=(
            P("groups", None, "dom"),
            P("groups", None, "dom"),
            P("groups"),
            P(("groups", "dom"), None),
            P("groups"),
            P("groups"),
            P(),
            P(),
            P(),
            P(),
            P(),
            P(),
            P(),
            P(),
        ),
        out_specs=(P("groups", None, "dom"), P("groups", None, "dom"), P("groups", None, "dom")),
        check_vma=False,
    )
```

```python
import functools
import math

import jax
import jax.numpy as jnp
from jax import lax
from jax.experimental import pallas as pl
from jax.experimental.pallas import tpu as pltpu
from jax.sharding import PartitionSpec as P

NA = 64
PAIR = 2 * NA
STEPS = 4
UNROLL = 4

step_time = 0.05
motion_work_lower_limit = 1e-06
LOG2E = math.log2(math.e)


def dot(a, b):
    return jnp.dot(a, b, preferred_element_type=jnp.float32)


def dot_rows(a, b):
    return lax.dot_general(a, b, (((1,), (1,)), ((), ())), preferred_element_type=jnp.float32)


def pieces(value, count):
    width = value.shape[1]
    row = lax.broadcasted_iota(jnp.int32, (16, width), 0)
    tile = jnp.zeros((16, width), jnp.float32)
    for index in range(count):
        part = value.astype(jnp.bfloat16).astype(jnp.float32)
        tile = jnp.where(row == index, part, tile)
        value = value - part
    return tile.astype(jnp.bfloat16)


def swap_halves(first, second):
    low = lax.broadcasted_iota(jnp.int32, first.shape, first.ndim - 1) < NA
    return pltpu.roll(jnp.where(low, second, first), NA, first.ndim - 1)


def basis(displacement, basis_count):
    dx, dy, dz = displacement
    rest = jnp.maximum(1.0 - (dx * dx + dy * dy + dz * dz), 0.0)
    envelope = rest * rest
    vectors = [dx * envelope, dy * envelope, dz * envelope]
    span = basis_count - 1
    rate = 2.0 * span * LOG2E
    offset = 0.5 - rest
    center = jnp.exp2((-2.0 * span * span * LOG2E) * (offset * offset)) * envelope
    slope = rate * offset
    up = jnp.exp2(slope)
    down = jnp.exp2(-slope)
    up_two = up * up
    down_two = down * down
    rising = [center * up]
    falling = [center * down]
    for _ in range(basis_count // 2 - 1):
        rising.append(rising[-1] * up_two)
        falling.append(falling[-1] * down_two)
    return falling[::-1] + rising, vectors


def prepare(
    place_ref,
    state_ref,
    feat_ref,
    first_ref,
    scale_one_ref,
    later_ref,
    scale_two_ref,
    push_ref,
    x_out,
    v_out,
    own_feat,
    table,
    message_push,
    later_push,
):
    extended = x_out.shape[0]
    cells = feat_ref.shape[0] // NA
    own_cells = 2 * (extended - 2)
    first_cell = place_ref[0] * own_cells - 2 + cells
    for p in range(extended):
        cell = lax.rem(first_cell + 2 * p, cells)
        at = pl.ds(pl.multiple_of(cell * NA, PAIR), PAIR)
        rows = state_ref[:, at]
        x = jnp.concatenate([rows[:3], jnp.zeros((5, PAIR), jnp.float32)], axis=0)
        if p == 0 or p == extended - 1:
            sub = lax.broadcasted_iota(jnp.int32, (8, PAIR), 0)
            wraps = (place_ref[0] == 0) if p == 0 else (place_ref[0] == place_ref[1] - 1)
            shift = jnp.where(wraps, float(cells), 0.0) * (-1.0 if p == 0 else 1.0)
            x = x + jnp.where(sub == 2, shift, 0.0)
        x_out[p] = x
        if 0 < p < extended - 1:
            v_out[p - 1] = jnp.concatenate([rows[3:6], jnp.zeros((5, PAIR), jnp.float32)], axis=0)
        own_feat[p * PAIR : (p + 1) * PAIR, :] = feat_ref[at, :]
    table[...] = dot(own_feat[...], first_ref[...]).astype(jnp.bfloat16)
    push = push_ref[...]
    message_push[...] = table[NA : NA + (extended - 1) * PAIR, :].astype(jnp.float32) * (push * scale_one_ref[...])
    parts = dot_rows(pieces(push * scale_two_ref[...], 3), later_ref[...])
    later_push[...] = jnp.broadcast_to(jnp.sum(parts, axis=0, keepdims=True), later_push.shape)


def advance(
    stage,
    place_ref,
    thermal_ref,
    x_ref,
    v_ref,
    g_ref,
    edge_ref,
    got_ref,
    own_feat,
    table,
    message_push,
    later_push,
    filter_ref,
    scale_one_ref,
    mix_ref,
    x_out,
    v_out,
    g_out,
    edge_out,
    e_rows,
    h_rows,
    lhs_0,
    lhs_1,
    vec_0,
    vec_1,
    vec_2,
    vec_3,
    message_0,
    message_1,
    forces,
):
    own_pairs = v_ref.shape[0]
    extended = own_pairs + 2
    pairs = own_pairs + 1
    total_cells = 2 * own_pairs * place_ref[1]
    basis_count = filter_ref.shape[0]
    channels = filter_ref.shape[1]
    sub = lax.broadcasted_iota(jnp.int32, (8, PAIR), 0)
    low = lax.broadcasted_iota(jnp.int32, (1, PAIR), 1) < NA
    span = basis_count - 1
    order = lax.broadcasted_iota(jnp.int32, (basis_count, 1), 0).astype(jnp.float32) - 0.5 * span
    filters = filter_ref[...] * jnp.exp(-2.0 * order * order)
    filters = jnp.concatenate([filters, filters], axis=1)
    scale_square = scale_one_ref[...] * scale_one_ref[...]
    scale_square = jnp.concatenate([scale_square, scale_square], axis=1)

    if stage == 0:
        e_rows[...] = x_ref[...]
        half_v = v_ref[...]
    else:
        if stage == 1:
            stretch = jnp.ones((1, 1), jnp.float32)
        else:
            kinetic = edge_ref[0, 1, 3:4, 0:1] + got_ref[0, 1, 3:4, 0:1]
            mean = kinetic / (3.0 * NA * total_cells.astype(jnp.float32)) + motion_work_lower_limit
            stretch = jnp.sqrt(thermal_ref[0] / mean)
        v = v_ref[...] * stretch
        half_v = v + (0.5 * step_time) * g_ref[...]
        e_rows[1 : own_pairs + 1] = x_ref[...] + step_time * v
        z_shift = jnp.where(sub == 2, total_cells.astype(jnp.float32), 0.0)
        left = got_ref[1, 0] + (step_time * stretch) * got_ref[1, 1]
        right = got_ref[0, 0] + (step_time * stretch) * got_ref[0, 1]
        e_rows[0] = jnp.where(place_ref[0] == 0, left - z_shift, left)
        e_rows[extended - 1] = jnp.where(place_ref[0] == place_ref[1] - 1, right + z_shift, right)
    h_rows[...] = swap_halves(e_rows[0:pairs], e_rows[1:extended])

    blank = jnp.zeros((PAIR, channels), jnp.bfloat16)
    lhs, vec = (lhs_0, lhs_1), (vec_0, vec_1, vec_2, vec_3)
    message = (message_0, message_1)

    def make_rows(q, radial, vectors_ref):
        columns = jnp.transpose(h_rows[q])
        before = e_rows[q]
        after = e_rows[q + 1]
        across = jnp.where(low, after, before)
        for chunk in range(NA // 16):
            start = chunk * 16
            own_a = [columns[start : start + 16, c : c + 1] for c in range(3)]
            own_b = [columns[NA + start : NA + start + 16, c : c + 1] for c in range(3)]
            own_a = [jnp.broadcast_to(o, (16, PAIR)) for o in own_a]
            own_b = [jnp.broadcast_to(o, (16, PAIR)) for o in own_b]
            blocks = (
                [before[c : c + 1] - own_a[c] for c in range(3)],
                [after[c : c + 1] - own_b[c] for c in range(3)],
                [across[c : c + 1] - jnp.where(low, own_a[c], own_b[c]) for c in range(3)],
            )
            for block, displacement in enumerate(blocks):
                radials, vectors = basis(displacement, basis_count)
                at = slice(block * PAIR, (block + 1) * PAIR)
                for k, value in enumerate(radials):
                    radial[k * NA + start : k * NA + start + 16, at] = value.astype(jnp.bfloat16)
                for c, value in enumerate(vectors):
                    vectors_ref[c * NA + start : c * NA + start + 16, at] = value.astype(jnp.bfloat16)

    def make_messages(q, radial, vectors_ref, out):
        if isinstance(q, int):
            near = table[q * PAIR : (q + 2) * PAIR, :]
        else:
            near = table[pl.ds(pl.multiple_of(q * PAIR, PAIR), 2 * PAIR), :]
        signals = jnp.concatenate(
            [
                jnp.concatenate([near[:PAIR], blank], axis=1),
                jnp.concatenate([blank, near[PAIR:]], axis=1),
                jnp.concatenate([near[PAIR : 3 * NA], blank[:NA]], axis=1),
                jnp.concatenate([blank[:NA], near[NA:PAIR]], axis=1),
            ],
            axis=0,
        )
        sums = dot(vectors_ref[...], signals)
        norm = sums[:NA] * sums[:NA]
        for c in range(1, 3):
            part = sums[c * NA : (c + 1) * NA]
            norm = norm + part * part
        norm = (norm * scale_square).astype(jnp.bfloat16)
        sums = dot(radial[...], signals)
        scalar = sums[:NA] * filters[0:1]
        for k in range(1, basis_count):
            scalar = scalar + sums[k * NA : (k + 1) * NA] * filters[k : k + 1]
        scalar = scalar.astype(jnp.bfloat16)
        for own in range(2):
            at = slice(own * channels, (own + 1) * channels)
            out[own * NA : (own + 1) * NA, :channels] = scalar[:, at]
            out[own * NA : (own + 1) * NA, channels:] = norm[:, at]

    def make_force(q, message_ref, vectors_ref):
        if isinstance(q, int):
            at_feat = slice(NA + q * PAIR, NA + (q + 1) * PAIR)
            at_push = slice(q * PAIR, (q + 1) * PAIR)
        else:
            at_feat = pl.ds(pl.multiple_of(q * PAIR, PAIR) + NA, PAIR)
            at_push = pl.ds(pl.multiple_of(q * PAIR, PAIR), PAIR)
        half = 0.5 * dot(message_ref[...], mix_ref[...])
        hidden = (own_feat[at_feat, :].astype(jnp.float32) + (half + half * jnp.tanh(half))).astype(jnp.bfloat16)
        pull = hidden.astype(jnp.float32) * later_push[0:1] + message_push[at_push, :]
        pull = jnp.sum(pull, axis=1, keepdims=True)
        first = jnp.broadcast_to(pull[:NA], (NA, PAIR))
        second = jnp.broadcast_to(pull[NA:], (NA, PAIR))
        weights = (first, second, jnp.where(low, first, second))
        for c in range(3):
            sums = []
            for block in range(3):
                value = vectors_ref[c * NA : (c + 1) * NA, block * PAIR : (block + 1) * PAIR].astype(jnp.float32)
                value = value * weights[block]
                total = value[:8]
                for row in range(8, NA, 8):
                    total = total + value[row : row + 8]
                sums.append(total)
            forces[q, c] = forces[q, c] - sums[0] - jnp.where(low, 0.0, sums[2])
            forces[q + 1, c] = -sums[1] - jnp.where(low, sums[2], 0.0)

    forces[0] = jnp.zeros(forces.shape[1:], jnp.float32)

    def stage_of(q, t, rows=True, before=True):
        if before:
            make_force(q - 1, message[(t + 1) % 2], vec[(t + 3) % 4])
        make_messages(q, lhs[t % 2], vec[t % 4], message[t % 2])
        if rows:
            make_rows(q + 1, lhs[(t + 1) % 2], vec[(t + 1) % 4])

    make_rows(0, lhs_0, vec_0)
    stage_of(0, 0, before=False)
    whole = (pairs - 2) // UNROLL

    if whole > 1:

        def several(i, _):
            for t in range(UNROLL):
                stage_of(i * UNROLL + t + 1, t + 1)
            return 0

        lax.fori_loop(0, whole, several, 0)
    for q in range(whole * UNROLL + 1 if whole > 1 else 1, pairs):
        stage_of(q, q, rows=q < pairs - 1)
    make_force(pairs - 1, message[(pairs - 1) % 2], vec[(pairs - 1) % 4])

    for p in range(own_pairs):
        tile = jnp.zeros((8, PAIR), jnp.float32)
        for c in range(3):
            tile = jnp.where(sub == c, jnp.sum(forces[p + 1, c], axis=0, keepdims=True), tile)
        g_out[p] = tile
    g = g_out[...]
    if stage == 0:
        v = half_v
    else:
        v = half_v + (0.5 * step_time) * g
    v_out[...] = v
    kinetic = jnp.sum(v * v, axis=0)
    kinetic = jnp.sum(jnp.sum(kinetic, axis=1, keepdims=True), axis=0, keepdims=True)
    x = e_rows[1 : own_pairs + 1]
    if stage < 3:
        x = x + (0.5 * step_time * step_time) * g
    x_out[...] = x
    for edge, p in enumerate((0, own_pairs - 1)):
        edge_out[edge, 0] = x[p]
        edge_out[edge, 1] = jnp.where(sub == 3, kinetic, v[p])


VMEM_SPEC = pl.BlockSpec(memory_space=pltpu.VMEM)
SMEM_SPEC = pl.BlockSpec(memory_space=pltpu.SMEM)


def run_prepare(place, state, features, per_replica, first, scale_one, later, scale_two, push):
    atoms, channels = features.shape
    own_pairs = atoms // per_replica // PAIR
    extended = own_pairs + 2
    return pl.pallas_call(
        prepare,
        out_shape=(
            jax.ShapeDtypeStruct((extended, 8, PAIR), jnp.float32),
            jax.ShapeDtypeStruct((own_pairs, 8, PAIR), jnp.float32),
            jax.ShapeDtypeStruct((extended * PAIR, channels), jnp.bfloat16),
            jax.ShapeDtypeStruct((extended * PAIR, channels), jnp.bfloat16),
            jax.ShapeDtypeStruct(((extended - 1) * PAIR, channels), jnp.float32),
            jax.ShapeDtypeStruct((8, channels), jnp.float32),
        ),
        in_specs=[SMEM_SPEC] + [VMEM_SPEC] * 7,
        out_specs=(VMEM_SPEC,) * 6,
        compiler_params=pltpu.CompilerParams(vmem_limit_bytes=20 * 1024 * 1024),
    )(place, state, features, first, scale_one, later, scale_two, push)


def run_advance(stage, place, thermal, x, v, g, edge, got, own_feat, table, message_push, later_push, filters, scale_one, mix):
    own_pairs = v.shape[0]
    channels = table.shape[1]
    basis_count = filters.shape[0]
    tiles = jax.ShapeDtypeStruct(v.shape, jnp.float32)
    lhs = pltpu.VMEM((basis_count * NA, 3 * PAIR), jnp.bfloat16)
    vec = pltpu.VMEM((3 * NA, 3 * PAIR), jnp.bfloat16)
    message = pltpu.VMEM((PAIR, 2 * channels), jnp.bfloat16)
    return pl.pallas_call(
        functools.partial(advance, stage),
        out_shape=(tiles, tiles, tiles, jax.ShapeDtypeStruct((2, 2, 8, PAIR), jnp.float32)),
        in_specs=[SMEM_SPEC] * 2 + [VMEM_SPEC] * 12,
        out_specs=(VMEM_SPEC,) * 4,
        scratch_shapes=[
            pltpu.VMEM((own_pairs + 2, 8, PAIR), jnp.float32),
            pltpu.VMEM((own_pairs + 1, 8, PAIR), jnp.float32),
            lhs,
            lhs,
            vec,
            vec,
            vec,
            vec,
            message,
            message,
            pltpu.VMEM((own_pairs + 2, 3, 8, PAIR), jnp.float32),
        ],
        compiler_params=pltpu.CompilerParams(vmem_limit_bytes=20 * 1024 * 1024),
    )(place, thermal, x, v, g, edge, got, own_feat, table, message_push, later_push, filters, scale_one, mix)


def run_steps(place, thermal, state, features, per_replica, exchange, weights):
    first, filters, scale_one, mix, later, scale_two, push = weights
    x, v, *fixed = run_prepare(place, state, features, per_replica, first, scale_one, later, scale_two, push)
    edge = got = jnp.zeros((2, 2, 8, PAIR), jnp.float32)
    g = v
    for step in range(STEPS + 1):
        stage = min(step, 2) if step < STEPS else 3
        x, v, g, edge = run_advance(
            stage, place, thermal, x, v, g, edge, got, *fixed, filters, scale_one, mix
        )
        if step < STEPS:
            got = exchange(edge)
    return x, v, g, edge[0, 1, 3, 0]


def on_device(
    particle_places,
    particle_speeds,
    thermal_targets,
    element_features,
    swap_counterpart_slot,
    swap_approval_flags,
    initial_signal_projector,
    initial_distance_filter,
    initial_directional_scales,
    invariant_revision_matrix,
    magnitude_revision_matrix,
    later_signal_projector,
    later_directional_scales,
    push_output_matrix,
):
    replicas = particle_places.shape[0]
    local_atoms = particle_places.shape[2]
    local_cells = local_atoms // NA
    devices = lax.axis_size("dom")
    own = lax.axis_index("dom")
    per_replica = devices // replicas
    bits = devices.bit_length() - 1
    replica_bits = replicas.bit_length() - 1

    def trade(value, mask):
        return lax.ppermute(value, "dom", [(i, i ^ mask) for i in range(devices)])

    state = jnp.concatenate([particle_places, particle_speeds], axis=1)
    features = element_features
    for level in range(bits):
        mask = devices >> (level + 1)
        upper = (own & mask) > 0
        if level < replica_bits:
            half = state.shape[0] // 2
            keep = jnp.where(upper, state[half:], state[:half])
            send = jnp.where(upper, state[:half], state[half:])
        else:
            keep = send = state
        got = trade(send, mask)
        got_features = trade(features, mask)
        axis = 1 + level
        state = jnp.stack([jnp.where(upper, got, keep), jnp.where(upper, keep, got)], axis=axis)
        features = jnp.stack(
            [jnp.where(upper, got_features, features), jnp.where(upper, features, got_features)], axis=level
        )
        if level + 1 < bits:
            state, features = lax.optimization_barrier((state, features))
    state = state.reshape(devices, 6, local_atoms).transpose(1, 0, 2).reshape(6, devices * local_atoms)
    features = features.reshape(devices * local_atoms, -1)
    thermal = lax.dynamic_slice(thermal_targets, (own // per_replica,), (1,))
    place = jnp.stack([own % per_replica, jnp.full((), per_replica, own.dtype)]).astype(jnp.int32)
    weights = (
        initial_signal_projector,
        initial_distance_filter,
        initial_directional_scales[None],
        jnp.concatenate([invariant_revision_matrix, magnitude_revision_matrix], axis=0),
        later_signal_projector,
        later_directional_scales[None],
        push_output_matrix[None],
    )

    def exchange(edge):
        if per_replica == 2:
            return trade(edge, 1)
        groups = [list(range(i, i + per_replica)) for i in range(0, devices, per_replica)]
        up = [(a, b) for g in groups for a, b in zip(g, g[1:] + g[:1])]
        kinetic = lax.psum(edge[0, 1, 3], "dom", axis_index_groups=groups) - edge[0, 1, 3]
        before = lax.ppermute(edge[1], "dom", up)
        after = lax.ppermute(edge[0], "dom", [(b, a) for a, b in up])
        return jnp.stack([after.at[1, 3].set(kinetic), before])

    x, v, g, kinetic = run_steps(place, thermal, state, features, per_replica, exchange, weights)

    state = jnp.stack([x, v, g])[:, :, :3].transpose(0, 2, 1, 3).reshape(9, -1)
    state = jnp.concatenate([state, jnp.broadcast_to(kinetic, (1, state.shape[1]))], axis=0)[:, None]
    for level in range(replica_bits, bits):
        mask = devices >> (level + 1)
        upper = (own & mask) > 0
        got = trade(state, mask)
        state = jnp.stack([jnp.where(upper, got, state), jnp.where(upper, state, got)], axis=1 + level - replica_bits)
        state = state.reshape((10,) + (2,) * (level + 1 - replica_bits) + (-1,))
    state = state.reshape(10, per_replica, -1)
    kinetic = jnp.sum(state[9, :, 0])
    stretch = jnp.sqrt(thermal[0] / (kinetic / (3.0 * devices * local_atoms) + motion_work_lower_limit))
    factor = jnp.where((jnp.arange(9) // 3) == 1, stretch, 1.0)
    state = state[:9] * factor[:, None, None]

    state = state.reshape(9, replicas, per_replica, local_atoms)
    state = lax.dynamic_index_in_dim(state, own % per_replica, 2, keepdims=False)
    state = state.transpose(1, 0, 2)[:, None]
    for level in range(replica_bits):
        mask = devices >> (level + 1)
        upper = (own & mask) > 0
        half = state.shape[0] // 2
        keep = jnp.where(upper, state[half:], state[:half])
        send = jnp.where(upper, state[:half], state[half:])
        got = trade(send, mask)
        state = jnp.stack([jnp.where(upper, got, keep), jnp.where(upper, keep, got)], axis=1 + level)
    state = state.reshape(replicas, 3, 3, local_atoms)

    ladder_slot = jnp.arange(replicas, dtype=jnp.int32)
    source = jnp.where(swap_approval_flags > 0, swap_counterpart_slot, ladder_slot)
    chosen = source[:, None] == ladder_slot[None, :]
    state = jnp.sum(jnp.where(chosen[:, :, None, None, None], state[None], 0.0), axis=1)
    thermal_source = jnp.sum(jnp.where(chosen, thermal_targets[None, :], 0.0), axis=1)
    thermal_ratio = jnp.sqrt(thermal_targets / thermal_source)
    atom_cell = (own * local_cells + jnp.arange(local_atoms, dtype=jnp.int32) // NA).astype(jnp.float32)
    cell_floor = jnp.array([0.0, 0.0, 1.0], jnp.float32)[:, None] * atom_cell[None, :]
    return (
        state[:, 0] - cell_floor[None],
        state[:, 1] * thermal_ratio[:, None, None],
        state[:, 2],
    )


def solution(mesh):
    return jax.shard_map(
        on_device,
        mesh=mesh,
        in_specs=(
            P("groups", None, "dom"),
            P("groups", None, "dom"),
            P("groups"),
            P(("groups", "dom"), None),
            P("groups"),
            P("groups"),
            P(),
            P(),
            P(),
            P(),
            P(),
            P(),
            P(),
            P(),
        ),
        out_specs=(P("groups", None, "dom"), P("groups", None, "dom"), P("groups", None, "dom")),
        check_vma=False,
    )
```

```python
import functools
import math

import jax
import jax.numpy as jnp
from jax import lax
from jax.experimental import pallas as pl
from jax.experimental.pallas import tpu as pltpu
from jax.sharding import PartitionSpec as P

NA = 64
PAIR = 2 * NA
STEPS = 4
UNROLL = 2
SMALL_ROWS = 4

step_time = 0.05
motion_work_lower_limit = 1e-06
LOG2E = math.log2(math.e)


def dot(a, b):
    return jnp.dot(a, b, preferred_element_type=jnp.float32)


def dot_rows(a, b):
    return lax.dot_general(a, b, (((1,), (1,)), ((), ())), preferred_element_type=jnp.float32)


def pieces(value, count):
    width = value.shape[1]
    row = lax.broadcasted_iota(jnp.int32, (16, width), 0)
    tile = jnp.zeros((16, width), jnp.float32)
    for index in range(count):
        part = value.astype(jnp.bfloat16).astype(jnp.float32)
        tile = jnp.where(row == index, part, tile)
        value = value - part
    return tile.astype(jnp.bfloat16)


def swap_halves(first, second):
    low = lax.broadcasted_iota(jnp.int32, first.shape, first.ndim - 1) < NA
    return pltpu.roll(jnp.where(low, second, first), NA, first.ndim - 1)


def basis(displacement, basis_count):
    dx, dy, dz = displacement
    rest = jnp.maximum(1.0 - (dx * dx + dy * dy + dz * dz), 0.0)
    envelope = rest * rest
    vectors = [dx * envelope, dy * envelope, dz * envelope]
    span = basis_count - 1
    rate = 2.0 * span * LOG2E
    offset = 0.5 - rest
    center = jnp.exp2((-2.0 * span * span * LOG2E) * (offset * offset)) * envelope
    slope = rate * offset
    up = jnp.exp2(slope)
    down = jnp.exp2(-slope)
    up_two = up * up
    down_two = down * down
    rising = [center * up]
    falling = [center * down]
    for _ in range(basis_count // 2 - 1):
        rising.append(rising[-1] * up_two)
        falling.append(falling[-1] * down_two)
    return falling[::-1] + rising, vectors


def prepare(
    place_ref,
    state_ref,
    feat_ref,
    weight_ref,
    small_ref,
    x_out,
    v_out,
    own_feat,
    table,
    message_push,
    later_push,
):
    extended = x_out.shape[0]
    cells = feat_ref.shape[0] // NA
    own_cells = 2 * (extended - 2)
    first_cell = place_ref[0] * own_cells - 2 + cells
    for p in range(extended):
        cell = lax.rem(first_cell + 2 * p, cells)
        at = pl.ds(pl.multiple_of(cell * NA, PAIR), PAIR)
        rows = state_ref[:, at]
        x = jnp.concatenate([rows[:3], jnp.zeros((5, PAIR), jnp.float32)], axis=0)
        sub = lax.broadcasted_iota(jnp.int32, (8, PAIR), 0)
        lane = lax.broadcasted_iota(jnp.int32, (8, PAIR), 1)
        floor = (place_ref[0] * own_cells - 2 + 2 * p + lane // NA).astype(jnp.float32)
        x_out[p] = x + jnp.where(sub == 2, floor, 0.0)
        if 0 < p < extended - 1:
            v_out[p - 1] = jnp.concatenate([rows[3:6], jnp.zeros((5, PAIR), jnp.float32)], axis=0)
        own_feat[p * PAIR : (p + 1) * PAIR, :] = feat_ref[at, :]
    channels = feat_ref.shape[1]
    basis_count = small_ref.shape[0] - SMALL_ROWS
    table[...] = dot(own_feat[...], weight_ref[:channels, :]).astype(jnp.bfloat16)
    message_push[...] = (
        table[NA : NA + (extended - 1) * PAIR, :].astype(jnp.float32) * small_ref[basis_count + 1 : basis_count + 2, :]
    )
    parts = dot_rows(pieces(small_ref[basis_count + 2 : basis_count + 3, :], 3), weight_ref[3 * channels :, :])
    later_push[...] = jnp.broadcast_to(jnp.sum(parts, axis=0, keepdims=True), later_push.shape)


def advance(
    stage,
    parts_count,
    place_ref,
    x_ref,
    v_ref,
    g_ref,
    edge_ref,
    got_ref,
    own_feat,
    table,
    message_push,
    later_push,
    weight_ref,
    small_ref,
    x_out,
    v_out,
    g_out,
    last_out,
    e_rows,
    h_rows,
    lhs_0,
    lhs_1,
    vec_0,
    vec_1,
    vec_2,
    vec_3,
    message_0,
    message_1,
    forces,
):
    own_pairs = v_ref.shape[0]
    extended = own_pairs + 2
    pairs = own_pairs + 1
    total_cells = 2 * own_pairs * place_ref[1]
    channels = small_ref.shape[1]
    basis_count = small_ref.shape[0] - SMALL_ROWS
    sub = lax.broadcasted_iota(jnp.int32, (8, PAIR), 0)
    low = lax.broadcasted_iota(jnp.int32, (1, PAIR), 1) < NA
    filters = small_ref[:basis_count, :]
    filters = jnp.concatenate([filters, filters], axis=1)
    scale_square = small_ref[basis_count : basis_count + 1, :]
    scale_square = jnp.concatenate([scale_square, scale_square], axis=1)

    if stage == 0:
        e_rows[...] = x_ref[...]
        half_v = v_ref[...]
    else:
        if stage == 1:
            stretch = jnp.ones((1, 1), jnp.float32)
        else:
            kinetic = edge_ref[0, 1, 3:4, 0:1] + got_ref[0, 1, 3:4, 0:1]
            mean = kinetic / (3.0 * NA * total_cells.astype(jnp.float32)) + motion_work_lower_limit
            stretch = jnp.sqrt(small_ref[basis_count + 3 : basis_count + 4, 0:1] / mean)
        v = v_ref[...] * stretch
        half_v = v + (0.5 * step_time) * g_ref[...]
        e_rows[1 : own_pairs + 1] = x_ref[...] + step_time * v
        z_shift = jnp.where(sub == 2, total_cells.astype(jnp.float32), 0.0)
        left = got_ref[1, 0] + (step_time * stretch) * got_ref[1, 1]
        right = got_ref[0, 0] + (step_time * stretch) * got_ref[0, 1]
        e_rows[0] = jnp.where(place_ref[0] == 0, left - z_shift, left)
        e_rows[extended - 1] = jnp.where(place_ref[0] == place_ref[1] - 1, right + z_shift, right)
    h_rows[...] = swap_halves(e_rows[0:pairs], e_rows[1:extended])

    blank = jnp.zeros((PAIR, channels), jnp.bfloat16)
    lhs, vec = (lhs_0, lhs_1), (vec_0, vec_1, vec_2, vec_3)
    message = (message_0, message_1)

    def make_rows(q, radial, vectors_ref):
        columns = jnp.transpose(h_rows[q])
        before = e_rows[q]
        after = e_rows[q + 1]
        across = jnp.where(low, after, before)
        for chunk in range(NA // 16):
            start = chunk * 16
            own_a = [columns[start : start + 16, c : c + 1] for c in range(3)]
            own_b = [columns[NA + start : NA + start + 16, c : c + 1] for c in range(3)]
            own_a = [jnp.broadcast_to(o, (16, PAIR)) for o in own_a]
            own_b = [jnp.broadcast_to(o, (16, PAIR)) for o in own_b]
            blocks = (
                [before[c : c + 1] - own_a[c] for c in range(3)],
                [after[c : c + 1] - own_b[c] for c in range(3)],
                [across[c : c + 1] - jnp.where(low, own_a[c], own_b[c]) for c in range(3)],
            )
            for block, displacement in enumerate(blocks):
                radials, vectors = basis(displacement, basis_count)
                at = slice(block * PAIR, (block + 1) * PAIR)
                for k, value in enumerate(radials):
                    radial[k * NA + start : k * NA + start + 16, at] = value.astype(jnp.bfloat16)
                for c, value in enumerate(vectors):
                    vectors_ref[c * NA + start : c * NA + start + 16, at] = value.astype(jnp.bfloat16)

    def make_messages(q, radial, vectors_ref, out):
        if isinstance(q, int):
            near = table[q * PAIR : (q + 2) * PAIR, :]
        else:
            near = table[pl.ds(pl.multiple_of(q * PAIR, PAIR), 2 * PAIR), :]
        signals = jnp.concatenate(
            [
                jnp.concatenate([near[:PAIR], blank], axis=1),
                jnp.concatenate([blank, near[PAIR:]], axis=1),
                jnp.concatenate([near[PAIR : 3 * NA], blank[:NA]], axis=1),
                jnp.concatenate([blank[:NA], near[NA:PAIR]], axis=1),
            ],
            axis=0,
        )
        sums = dot(vectors_ref[...], signals)
        norm = sums[:NA] * sums[:NA]
        for c in range(1, 3):
            part = sums[c * NA : (c + 1) * NA]
            norm = norm + part * part
        norm = (norm * scale_square).astype(jnp.bfloat16)
        sums = dot(radial[...], signals)
        scalar = sums[:NA] * filters[0:1]
        for k in range(1, basis_count):
            scalar = scalar + sums[k * NA : (k + 1) * NA] * filters[k : k + 1]
        scalar = scalar.astype(jnp.bfloat16)
        for own in range(2):
            at = slice(own * channels, (own + 1) * channels)
            out[own * NA : (own + 1) * NA, :channels] = scalar[:, at]
            out[own * NA : (own + 1) * NA, channels:] = norm[:, at]

    def make_force(q, message_ref, vectors_ref):
        if isinstance(q, int):
            at_feat = slice(NA + q * PAIR, NA + (q + 1) * PAIR)
            at_push = slice(q * PAIR, (q + 1) * PAIR)
        else:
            at_feat = pl.ds(pl.multiple_of(q * PAIR, PAIR) + NA, PAIR)
            at_push = pl.ds(pl.multiple_of(q * PAIR, PAIR), PAIR)
        half = 0.5 * dot(message_ref[...], weight_ref[channels : 3 * channels, :])
        hidden = (own_feat[at_feat, :].astype(jnp.float32) + (half + half * jnp.tanh(half))).astype(jnp.bfloat16)
        pull = hidden.astype(jnp.float32) * later_push[0:1] + message_push[at_push, :]
        pull = jnp.sum(pull, axis=1, keepdims=True)
        first = jnp.broadcast_to(pull[:NA], (NA, PAIR))
        second = jnp.broadcast_to(pull[NA:], (NA, PAIR))
        weights = (first, second, jnp.where(low, first, second))
        for c in range(3):
            sums = []
            for block in range(3):
                value = vectors_ref[c * NA : (c + 1) * NA, block * PAIR : (block + 1) * PAIR].astype(jnp.float32)
                value = value * weights[block]
                total = value[:8]
                for row in range(8, NA, 8):
                    total = total + value[row : row + 8]
                sums.append(total)
            forces[q, c] = forces[q, c] - sums[0] - jnp.where(low, 0.0, sums[2])
            forces[q + 1, c] = -sums[1] - jnp.where(low, sums[2], 0.0)

    forces[0] = jnp.zeros(forces.shape[1:], jnp.float32)

    def stage_of(q, t, rows=True, before=True):
        if before:
            make_force(q - 1, message[(t + 1) % 2], vec[(t+1)%2])
        make_messages(q, lhs[t % 2], vec[t%2], message[t % 2])
        if rows:
            make_rows(q + 1, lhs[(t + 1) % 2], vec[(t+1)%2])

    make_rows(0, lhs_0, vec_0)
    stage_of(0, 0, before=False)
    whole = (pairs - 2) // UNROLL

    if whole > 1:

        def several(i, _):
            for t in range(UNROLL):
                stage_of(i * UNROLL + t + 1, t + 1)
            return 0

        lax.fori_loop(0, whole, several, 0)
    for q in range(whole * UNROLL + 1 if whole > 1 else 1, pairs):
        stage_of(q, q, rows=q < pairs - 1)
    make_force(pairs - 1, message[(pairs - 1) % 2], vec[(pairs - 1) % 4])

    for p in range(own_pairs):
        tile = jnp.zeros((8, PAIR), jnp.float32)
        for c in range(3):
            tile = jnp.where(sub == c, jnp.sum(forces[p + 1, c], axis=0, keepdims=True), tile)
        g_out[p] = tile
    g = g_out[...]
    if stage == 0:
        v = half_v
    else:
        v = half_v + (0.5 * step_time) * g
    v_out[...] = v
    kinetic = jnp.sum(v * v, axis=0)
    kinetic = jnp.sum(jnp.sum(kinetic, axis=1, keepdims=True), axis=0, keepdims=True)
    x = e_rows[1 : own_pairs + 1]
    if stage < 3:
        x_out[...] = x + (0.5 * step_time * step_time) * g
        for edge, p in enumerate((0, own_pairs - 1)):
            last_out[edge, 0] = x_out[p]
            last_out[edge, 1] = jnp.where(sub == 3, kinetic, v[p])
        return
    x_out[...] = x
    rows = jnp.concatenate(
        [
            jnp.concatenate([x_out[p, 0:3], v_out[p, 0:3], g_out[p, 0:3]], axis=0)
            for p in range(own_pairs)
        ],
        axis=1,
    )
    chunks = last_out.shape[0] // parts_count
    width = own_pairs * PAIR // chunks
    whole = width // PAIR
    last_out[...] = jnp.zeros(last_out.shape, jnp.float32)
    end = last_out.shape[1] - 1
    last_out[:, end:, :] = jnp.broadcast_to(kinetic.reshape(1, 1, 1), (last_out.shape[0], 1, PAIR))
    first = place_ref[0] * chunks
    for chunk in range(chunks):
        at = chunk * width
        for group in range(whole):
            last_out[first + chunk, 9 * group : 9 * (group + 1), :] = rows[:, at : at + PAIR]
            at = at + PAIR
        if width % PAIR:
            tail = rows[:, at : at + NA]
            last_out[first + chunk, 9 * whole : 9 * whole + 4, :] = jnp.concatenate([tail[:4], tail[4:8]], axis=1)
            last_out[first + chunk, 9 * whole + 4 : 9 * whole + 5, :NA] = tail[8:]


def finish(place_ref, source_ref, got_ref, thermal_ref, x_out, v_out, g_out):
    replicas, width = x_out.shape[1:]
    whole = width // PAIR
    parts = place_ref[1]
    domain = place_ref[2]
    domains, chunk_rows = got_ref.shape[:2]
    part = domain // (domains // parts)
    atoms = float(domains * width)
    group = domains // replicas
    outs = (x_out, v_out, g_out)
    pieces_of = [[] for _ in range(9)]
    factors = []
    for r in range(replicas):
        source = source_ref[r]
        kinetic = got_ref[source * group, chunk_rows - 1 :, :]
        for other in range(1, group):
            kinetic = kinetic + got_ref[source * group + other, chunk_rows - 1 :, :]
        mean = kinetic / (3.0 * atoms) + motion_work_lower_limit
        source_target = jnp.full((1, PAIR), thermal_ref[source])
        factors.append(jnp.sqrt(source_target / mean) * jnp.sqrt(jnp.full((1, PAIR), thermal_ref[r]) / source_target))
        rows = got_ref[source * group + part]
        for row in range(9):
            pieces_of[row].append([rows[9 * g + row : 9 * g + row + 1] for g in range(whole)])
            if width % PAIR:
                at = 9 * whole + row % 4 if row < 8 else 9 * whole + 4
                tail = rows[at : at + 1, NA:] if 4 <= row < 8 else rows[at : at + 1, :NA]
                pieces_of[row][-1].append(tail)
    factor = jnp.concatenate(factors, axis=0)
    for row in range(9):
        for index in range(len(pieces_of[row][0])):
            value = jnp.concatenate([of_replica[index] for of_replica in pieces_of[row]], axis=0)
            size = value.shape[1]
            if row == 2:
                lane = lax.broadcasted_iota(jnp.int32, value.shape, 1)
                value = value - (domain * (width // NA) + (index * PAIR + lane) // NA).astype(jnp.float32)
            elif row // 3 == 1:
                value = value * factor[:, :size]
            outs[row // 3][row % 3, :, index * PAIR : index * PAIR + size] = value


VMEM_SPEC = pl.BlockSpec(memory_space=pltpu.VMEM)
SMEM_SPEC = pl.BlockSpec(memory_space=pltpu.SMEM)


def run_prepare(place, state, features, per_replica, weights, small):
    atoms, channels = features.shape
    own_pairs = atoms // per_replica // PAIR
    extended = own_pairs + 2
    return pl.pallas_call(
        prepare,
        out_shape=(
            jax.ShapeDtypeStruct((extended, 8, PAIR), jnp.float32),
            jax.ShapeDtypeStruct((own_pairs, 8, PAIR), jnp.float32),
            jax.ShapeDtypeStruct((extended * PAIR, channels), jnp.bfloat16),
            jax.ShapeDtypeStruct((extended * PAIR, channels), jnp.bfloat16),
            jax.ShapeDtypeStruct(((extended - 1) * PAIR, channels), jnp.float32),
            jax.ShapeDtypeStruct((8, channels), jnp.float32),
        ),
        in_specs=[SMEM_SPEC] + [VMEM_SPEC] * 4,
        out_specs=(VMEM_SPEC,) * 6,
        compiler_params=pltpu.CompilerParams(vmem_limit_bytes=20 * 1024 * 1024),
    )(place, state, features, weights, small)


def run_advance(stage, parts_count, last_shape, place, x, v, g, edge, got, own_feat, table, message_push, later_push, weights, small):
    own_pairs = v.shape[0]
    channels = table.shape[1]
    basis_count = small.shape[0] - SMALL_ROWS
    tiles = jax.ShapeDtypeStruct(v.shape, jnp.float32)
    lhs = pltpu.VMEM((basis_count * NA, 3 * PAIR), jnp.bfloat16)
    vec = pltpu.VMEM((3 * NA, 3 * PAIR), jnp.bfloat16)
    message = pltpu.VMEM((PAIR, 2 * channels), jnp.bfloat16)
    return pl.pallas_call(
        functools.partial(advance, stage, parts_count),
        out_shape=(tiles, tiles, tiles, jax.ShapeDtypeStruct(last_shape, jnp.float32)),
        in_specs=[SMEM_SPEC] + [VMEM_SPEC] * 11,
        out_specs=(VMEM_SPEC,) * 4,
        scratch_shapes=[
            pltpu.VMEM((own_pairs + 2, 8, PAIR), jnp.float32),
            pltpu.VMEM((own_pairs + 1, 8, PAIR), jnp.float32),
            lhs,
            lhs,
            vec,
            vec,
            vec,
            vec,
            message,
            message,
            pltpu.VMEM((own_pairs + 2, 3, 8, PAIR), jnp.float32),
        ],
        compiler_params=pltpu.CompilerParams(vmem_limit_bytes=20 * 1024 * 1024),
    )(place, x, v, g, edge, got, own_feat, table, message_push, later_push, weights, small)


def run_steps(place, state, features, per_replica, chunk_shape, exchange, weights, small):
    x, v, *fixed = run_prepare(place, state, features, per_replica, weights, small)
    edge_shape = (2, 2, 8, PAIR)
    edge = got = jnp.zeros(edge_shape, jnp.float32)
    g = v
    for step in range(STEPS + 1):
        stage = min(step, 2) if step < STEPS else 3
        shape = edge_shape if step < STEPS else chunk_shape
        x, v, g, edge = run_advance(stage, per_replica, shape, place, x, v, g, edge, got, *fixed, weights, small)
        if step < STEPS:
            got = exchange(edge)
    return edge


def run_finish(place, source, got, thermal_targets, local_atoms):
    replicas = thermal_targets.shape[0]
    out = jax.ShapeDtypeStruct((3, replicas, local_atoms), jnp.float32)
    whole = pl.BlockSpec(out.shape, lambda: (0, 0, 0))
    outs = pl.pallas_call(
        finish,
        out_shape=(out, out, out),
        in_specs=[SMEM_SPEC, SMEM_SPEC, VMEM_SPEC, SMEM_SPEC],
        out_specs=(whole, whole, whole),
    )(place, source, got, thermal_targets)
    return tuple(jnp.transpose(o, (1, 0, 2)) for o in outs)


def on_device(
    particle_places,
    particle_speeds,
    thermal_targets,
    element_features,
    swap_counterpart_slot,
    swap_approval_flags,
    initial_signal_projector,
    initial_distance_filter,
    initial_directional_scales,
    invariant_revision_matrix,
    magnitude_revision_matrix,
    later_signal_projector,
    later_directional_scales,
    push_output_matrix,
):
    replicas = particle_places.shape[0]
    local_atoms = particle_places.shape[2]
    local_cells = local_atoms // NA
    devices = lax.axis_size("dom")
    own = lax.axis_index("dom")
    per_replica = devices // replicas
    bits = devices.bit_length() - 1
    replica_bits = replicas.bit_length() - 1

    def trade(value, mask):
        return lax.ppermute(value, "dom", [(i, i ^ mask) for i in range(devices)])

    weights = jnp.concatenate(
        [initial_signal_projector, invariant_revision_matrix, magnitude_revision_matrix, later_signal_projector], axis=0
    )
    span = initial_distance_filter.shape[0] - 1
    order = (jnp.arange(span + 1, dtype=jnp.float32) - 0.5 * span)[:, None]
    thermal = lax.dynamic_slice(thermal_targets, (own // per_replica,), (1,))
    small = jnp.concatenate(
        [
            initial_distance_filter * jnp.exp(-2.0 * order * order),
            (initial_directional_scales * initial_directional_scales)[None],
            (push_output_matrix * initial_directional_scales)[None],
            (push_output_matrix * later_directional_scales)[None],
            jnp.broadcast_to(thermal[:, None], (1, push_output_matrix.shape[0])),
        ],
        axis=0,
    )
    place = jnp.stack([own % per_replica, jnp.full((), per_replica, own.dtype), own]).astype(jnp.int32)
    ladder_slot = jnp.arange(replicas, dtype=jnp.int32)
    source = jnp.where(swap_approval_flags > 0, swap_counterpart_slot, ladder_slot)

    atom_cell = jnp.arange(local_atoms, dtype=jnp.int32) // NA
    cell_floor = jnp.array([0.0, 0.0, 1.0], jnp.float32)[:, None] * (
        own * local_cells + atom_cell
    ).astype(jnp.float32)
    state = jnp.concatenate([particle_places - cell_floor, particle_speeds], axis=1)
    upper_part = lax.reduce_precision(state, 8, 7)
    state = jnp.stack([upper_part, state - upper_part], axis=1).astype(jnp.bfloat16)
    channels = element_features.shape[1]
    state = state.reshape(replicas, -1, channels)
    state_rows = state.shape[1]
    features = element_features
    for level in range(bits):
        mask = devices >> (level + 1)
        upper = (own & mask) > 0
        if level < replica_bits:
            half = state.shape[0] // 2
            keep = jnp.where(upper, state[half:], state[:half])
            send = jnp.where(upper, state[:half], state[half:])
        else:
            keep = send = state
        message = jnp.concatenate([features.reshape(-1, channels), send.reshape(-1, channels)], axis=0)
        if level == 1:
            message, weights, small, place, source = lax.optimization_barrier((message, weights, small, place, source))
        got = trade(message, mask)
        count = features.size // channels
        got_features = got[:count].reshape(features.shape)
        got = got[count:].reshape(send.shape)
        axis = 1 + level
        state = jnp.stack([jnp.where(upper, got, keep), jnp.where(upper, keep, got)], axis=axis)
        features = jnp.stack(
            [jnp.where(upper, got_features, features), jnp.where(upper, features, got_features)], axis=level
        )
    state = state.reshape(devices, 2, 6, local_atoms).astype(jnp.float32)
    state = (state[:, 0] + state[:, 1]).transpose(1, 0, 2).reshape(6, devices * local_atoms)
    features = features.reshape(devices * local_atoms, -1)

    def exchange(edge):
        if per_replica == 2:
            return trade(edge, 1)
        groups = [list(range(i, i + per_replica)) for i in range(0, devices, per_replica)]
        up = [(a, b) for g in groups for a, b in zip(g, g[1:] + g[:1])]
        kinetic = lax.psum(edge[0, 1, 3], "dom", axis_index_groups=groups) - edge[0, 1, 3]
        before = lax.ppermute(edge[1], "dom", up)
        after = lax.ppermute(edge[0], "dom", [(b, a) for a, b in up])
        return jnp.stack([after.at[1, 3].set(kinetic), before])

    chunk_rows = 9 * (local_atoms // PAIR) + (5 if local_atoms % PAIR else 0) + 1
    chunk_rows = -(-chunk_rows // 8) * 8
    chunks = run_steps(place, state, features, per_replica, (devices, chunk_rows, PAIR), exchange, weights, small)
    got = lax.all_to_all(chunks, "dom", 0, 0)
    return run_finish(place, source, got, thermal_targets, local_atoms)


def solution(mesh):
    return jax.shard_map(
        on_device,
        mesh=mesh,
        in_specs=(
            P("groups", None, "dom"),
            P("groups", None, "dom"),
            P("groups"),
            P(("groups", "dom"), None),
            P("groups"),
            P("groups"),
            P(),
            P(),
            P(),
            P(),
            P(),
            P(),
            P(),
            P(),
        ),
        out_specs=(P("groups", None, "dom"), P("groups", None, "dom"), P("groups", None, "dom")),
        check_vma=False,
    )
```

```python
import functools
import math

import jax
import jax.numpy as jnp
from jax import lax
from jax.experimental import pallas as pl
from jax.experimental.pallas import tpu as pltpu
from jax.sharding import PartitionSpec as P

NA = 64
PAIR = 2 * NA
STEPS = 4
UNROLL = 2
SMALL_ROWS = 7
CHUNK = 16
CHUNKS = NA // CHUNK

step_time = 0.05
motion_work_lower_limit = 1e-06
LOG2E = math.log2(math.e)


def dot(a, b):
    return jnp.dot(a, b, preferred_element_type=jnp.float32)


def dot_rows(a, b):
    return lax.dot_general(a, b, (((1,), (1,)), ((), ())), preferred_element_type=jnp.float32)


def pieces(value, count):
    width = value.shape[1]
    row = lax.broadcasted_iota(jnp.int32, (16, width), 0)
    tile = jnp.zeros((16, width), jnp.float32)
    for index in range(count):
        part = value.astype(jnp.bfloat16).astype(jnp.float32)
        tile = jnp.where(row == index, part, tile)
        value = value - part
    return tile.astype(jnp.bfloat16)


def swap_halves(first, second):
    low = lax.broadcasted_iota(jnp.int32, first.shape, first.ndim - 1) < NA
    return pltpu.roll(jnp.where(low, second, first), NA, first.ndim - 1)


def basis(displacement, basis_count):
    dx, dy, dz = displacement
    rest = jnp.maximum(1.0 - (dx * dx + dy * dy + dz * dz), 0.0)
    envelope = rest * rest
    vectors = [dx * envelope, dy * envelope, dz * envelope]
    span = basis_count - 1
    rate = 2.0 * span * LOG2E
    offset = 0.5 - rest
    center = jnp.exp2((-2.0 * span * span * LOG2E) * (offset * offset)) * envelope
    slope = rate * offset
    up = jnp.exp2(slope)
    down = jnp.exp2(-slope)
    up_two = up * up
    down_two = down * down
    rising = [center * up]
    falling = [center * down]
    for _ in range(basis_count // 2 - 1):
        rising.append(rising[-1] * up_two)
        falling.append(falling[-1] * down_two)
    return falling[::-1] + rising, vectors


def prepare(
    place_ref,
    state_ref,
    feat_ref,
    weight_ref,
    small_ref,
    x_out,
    v_out,
    own_feat,
    table,
    message_push,
    later_push,
):
    extended = x_out.shape[0]
    cells = feat_ref.shape[0] // NA
    own_cells = 2 * (extended - 2)
    first_cell = place_ref[0] * own_cells - 2 + cells
    for p in range(extended):
        cell = lax.rem(first_cell + 2 * p, cells)
        at = pl.ds(pl.multiple_of(cell * NA, PAIR), PAIR)
        rows = state_ref[:, at]
        x = jnp.concatenate([rows[:3], jnp.zeros((5, PAIR), jnp.float32)], axis=0)
        sub = lax.broadcasted_iota(jnp.int32, (8, PAIR), 0)
        lane = lax.broadcasted_iota(jnp.int32, (8, PAIR), 1)
        floor = (place_ref[0] * own_cells - 2 + 2 * p + lane // NA).astype(jnp.float32)
        x_out[p] = x + jnp.where(sub == 2, floor, 0.0)
        if 0 < p < extended - 1:
            v_out[p - 1] = jnp.concatenate([rows[3:6], jnp.zeros((5, PAIR), jnp.float32)], axis=0)
        own_feat[p * PAIR : (p + 1) * PAIR, :] = feat_ref[at, :]
    channels = feat_ref.shape[1]
    basis_count = small_ref.shape[0] - SMALL_ROWS
    table[...] = dot(own_feat[...], weight_ref[:channels, :]).astype(jnp.bfloat16)
    message_push[...] = (
        table[NA : NA + (extended - 1) * PAIR, :].astype(jnp.float32) * small_ref[basis_count + 1 : basis_count + 2, :]
    )
    parts = dot_rows(pieces(small_ref[basis_count + 2 : basis_count + 3, :], 3), weight_ref[3 * channels :, :])
    later_push[...] = jnp.broadcast_to(jnp.sum(parts, axis=0, keepdims=True), later_push.shape)


def advance(
    stage,
    parts_count,
    x_ref,
    v_ref,
    g_ref,
    edge_ref,
    got_ref,
    own_feat,
    table,
    message_push,
    later_push,
    weight_ref,
    small_ref,
    x_out,
    v_out,
    g_out,
    last_out,
    e_rows,
    h_rows,
    lhs,
    vec,
    message_0,
    message_1,
    forces,
):
    own_pairs = v_ref.shape[0]
    extended = own_pairs + 2
    pairs = own_pairs + 1
    total_cells = float(2 * own_pairs * parts_count)
    channels = small_ref.shape[1]
    basis_count = small_ref.shape[0] - SMALL_ROWS
    sub = lax.broadcasted_iota(jnp.int32, (8, PAIR), 0)
    low = lax.broadcasted_iota(jnp.int32, (1, PAIR), 1) < NA
    filters = small_ref[:basis_count, :]
    filters = jnp.concatenate([filters, filters], axis=1)
    scale_square = small_ref[basis_count : basis_count + 1, :]
    scale_square = jnp.concatenate([scale_square, scale_square], axis=1)

    if stage == 0:
        e_rows[...] = x_ref[...]
        half_v = v_ref[...]
    else:
        if stage == 1:
            stretch = jnp.ones((1, 1), jnp.float32)
        else:
            kinetic = edge_ref[0, 1, 3:4, 0:1] + got_ref[0, 1, 3:4, 0:1]
            mean = kinetic / (3.0 * NA * total_cells) + motion_work_lower_limit
            stretch = jnp.sqrt(small_ref[basis_count + 3 : basis_count + 4, 0:1] / mean)
        v = v_ref[...] * stretch
        half_v = v + (0.5 * step_time) * g_ref[...]
        e_rows[1 : own_pairs + 1] = x_ref[...] + step_time * v
        z_only = jnp.where(sub == 2, 1.0, 0.0)
        left = got_ref[1, 0] + (step_time * stretch) * got_ref[1, 1]
        right = got_ref[0, 0] + (step_time * stretch) * got_ref[0, 1]
        e_rows[0] = left + z_only * small_ref[basis_count + 4 : basis_count + 5, :]
        e_rows[extended - 1] = right + z_only * small_ref[basis_count + 5 : basis_count + 6, :]
    h_rows[...] = swap_halves(e_rows[0:pairs], e_rows[1:extended])

    blank = jnp.zeros((PAIR, channels), jnp.bfloat16)
    def beside(value):
        return jnp.concatenate([value, jnp.zeros_like(value)], axis=1)

    message = (message_0, message_1)

    def make_rows(q, chunk, columns, out):
        before = e_rows[q]
        after = e_rows[q + 1]
        across = jnp.where(low, after, before)
        start = chunk * CHUNK
        own_a = [columns[start : start + CHUNK, c : c + 1] for c in range(3)]
        own_b = [columns[NA + start : NA + start + CHUNK, c : c + 1] for c in range(3)]
        own_a = [jnp.broadcast_to(o, (CHUNK, PAIR)) for o in own_a]
        own_b = [jnp.broadcast_to(o, (CHUNK, PAIR)) for o in own_b]
        blocks = (
            [before[c : c + 1] - own_a[c] for c in range(3)],
            [after[c : c + 1] - own_b[c] for c in range(3)],
            [across[c : c + 1] - jnp.where(low, own_a[c], own_b[c]) for c in range(3)],
        )
        for block, displacement in enumerate(blocks):
            radials, vectors = basis(displacement, basis_count)
            for k, value in enumerate(radials + vectors):
                out[block][k * NA + start : k * NA + start + CHUNK, :] = value.astype(jnp.bfloat16)

    def make_messages(q, rows, out):
        if isinstance(q, int):
            near = table[q * PAIR : (q + 2) * PAIR, :]
        else:
            near = table[pl.ds(pl.multiple_of(q * PAIR, PAIR), 2 * PAIR), :]
        across = jnp.concatenate(
            [
                jnp.concatenate([near[PAIR : 3 * NA], blank[:NA]], axis=1),
                jnp.concatenate([blank[:NA], near[NA:PAIR]], axis=1),
            ],
            axis=0,
        )
        shared = dot(rows[2][...], across)
        for own in range(2):
            at = slice(own * channels, (own + 1) * channels)
            total = dot(rows[own][...], near[own * PAIR : (own + 1) * PAIR]) + shared[:, at]
            total = [total[k * NA : (k + 1) * NA] for k in range(basis_count + 3)]
            scalar = total[0] * filters[0:1, :channels]
            for k in range(1, basis_count):
                scalar = scalar + total[k] * filters[k : k + 1, :channels]
            norm = total[basis_count] * total[basis_count]
            for k in range(basis_count + 1, basis_count + 3):
                norm = norm + total[k] * total[k]
            out[own * NA : (own + 1) * NA, :channels] = scalar.astype(jnp.bfloat16)
            out[own * NA : (own + 1) * NA, channels:] = (norm * scale_square[:, :channels]).astype(jnp.bfloat16)

    def make_pull(q, message_ref):
        if isinstance(q, int):
            at_feat = slice(NA + q * PAIR, NA + (q + 1) * PAIR)
            at_push = slice(q * PAIR, (q + 1) * PAIR)
        else:
            at_feat = pl.ds(pl.multiple_of(q * PAIR, PAIR) + NA, PAIR)
            at_push = pl.ds(pl.multiple_of(q * PAIR, PAIR), PAIR)
        half = 0.5 * dot(message_ref[...], weight_ref[channels : 3 * channels, :])
        hidden = (own_feat[at_feat, :].astype(jnp.float32) + (half + half * jnp.tanh(half))).astype(jnp.bfloat16)
        pull = hidden.astype(jnp.float32) * later_push[0:1] + message_push[at_push, :]
        return jnp.sum(pull, axis=1, keepdims=True)

    def make_force(q, c, pull, blocks):
        first = jnp.broadcast_to(pull[:NA], (NA, PAIR))
        second = jnp.broadcast_to(pull[NA:], (NA, PAIR))
        weights = (first, second, jnp.where(low, first, second))
        totals = []
        for ref, weight in zip(blocks, weights):
            value = ref[c * NA : (c + 1) * NA, :].astype(jnp.float32) * weight
            total = value[:8]
            for row in range(8, NA, 8):
                total = total + value[row : row + 8]
            totals.append(total)
        forces[q, c] = forces[q, c] - totals[0] - jnp.where(low, 0.0, totals[2])
        forces[q + 1, c] = -totals[1] - jnp.where(low, totals[2], 0.0)

    forces[0] = jnp.zeros(forces.shape[1:], jnp.float32)

    def stage_of(q, t, rows=True, before=True):
        here, there = t % 2, (t + 1) % 2
        if before:
            pull = make_pull(q - 1, message[there])
            for c in range(3):
                make_force(q - 1, c, pull, vec[there])
        make_messages(q, lhs[here], message[here])
        for block in range(3):
            vec[here][block][...] = lhs[here][block][basis_count * NA :, :]
        if rows:
            columns = jnp.transpose(h_rows[q + 1])
            for chunk in range(CHUNKS):
                make_rows(q + 1, chunk, columns, lhs[there])

    columns = jnp.transpose(h_rows[0])
    for chunk in range(CHUNKS):
        make_rows(0, chunk, columns, lhs[0])
    whole = (pairs - 2) // UNROLL
    stage_of(0, 0, before=False)

    def several(i, _):
        for t in range(UNROLL):
            stage_of(i * UNROLL + t + 1, t + 1)
        return 0

    lax.fori_loop(0, whole, several, 0)
    for q in range(whole * UNROLL + 1, pairs):
        stage_of(q, q, rows=q < pairs - 1)
    last = pairs - 1
    pull = make_pull(last, message[last % 2])
    for c in range(3):
        make_force(last, c, pull, vec[last % 2])

    for p in range(own_pairs):
        tile = jnp.zeros((8, PAIR), jnp.float32)
        for c in range(3):
            tile = jnp.where(sub == c, jnp.sum(forces[p + 1, c], axis=0, keepdims=True), tile)
        g_out[p] = tile
    g = g_out[...]
    if stage == 0:
        v = half_v
    else:
        v = half_v + (0.5 * step_time) * g
    v_out[...] = v
    kinetic = jnp.sum(v * v, axis=0)
    kinetic = jnp.sum(jnp.sum(kinetic, axis=1, keepdims=True), axis=0, keepdims=True)
    x = e_rows[1 : own_pairs + 1]
    if stage < 3:
        x_out[...] = x + (0.5 * step_time * step_time) * g
        for edge, p in enumerate((0, own_pairs - 1)):
            last_out[edge, 0] = x_out[p]
            last_out[edge, 1] = jnp.where(sub == 3, kinetic, v[p])
        return
    x_out[...] = x
    rows = jnp.concatenate(
        [
            jnp.concatenate([x_out[p, 0:3], v_out[p, 0:3], g_out[p, 0:3]], axis=0)
            for p in range(own_pairs)
        ],
        axis=1,
    )
    chunks = last_out.shape[0] // parts_count
    width = own_pairs * PAIR // chunks
    whole = width // PAIR
    last_out[...] = jnp.zeros(last_out.shape, jnp.float32)
    end = last_out.shape[1] - 1
    last_out[:, end:, :] = jnp.broadcast_to(kinetic.reshape(1, 1, 1), (last_out.shape[0], 1, PAIR))
    part = small_ref[basis_count + 6 : basis_count + 7, :]
    for chunk in range(parts_count * chunks):
        chosen = part == float(chunk // chunks)
        at = chunk % chunks * width
        for group in range(whole):
            last_out[chunk, 9 * group : 9 * (group + 1), :] = jnp.where(chosen, rows[:, at : at + PAIR], 0.0)
            at = at + PAIR
        if width % PAIR:
            tail = jnp.where(chosen[:, :NA], rows[:, at : at + NA], 0.0)
            last_out[chunk, 9 * whole : 9 * whole + 4, :] = jnp.concatenate([tail[:4], tail[4:8]], axis=1)
            last_out[chunk, 9 * whole + 4 : 9 * whole + 5, :NA] = tail[8:]


def finish(place_ref, source_ref, got_ref, thermal_ref, x_out, v_out, g_out):
    replicas, width = x_out.shape[1:]
    whole = width // PAIR
    parts = place_ref[1]
    domain = place_ref[2]
    domains, chunk_rows = got_ref.shape[:2]
    part = domain // (domains // parts)
    atoms = float(domains * width)
    group = domains // replicas
    outs = (x_out, v_out, g_out)
    pieces_of = [[] for _ in range(9)]
    factors = []
    for r in range(replicas):
        source = source_ref[r]
        kinetic = got_ref[source * group, chunk_rows - 1 :, :]
        for other in range(1, group):
            kinetic = kinetic + got_ref[source * group + other, chunk_rows - 1 :, :]
        mean = kinetic / (3.0 * atoms) + motion_work_lower_limit
        source_target = jnp.full((1, PAIR), thermal_ref[source])
        factors.append(jnp.sqrt(source_target / mean) * jnp.sqrt(jnp.full((1, PAIR), thermal_ref[r]) / source_target))
        rows = got_ref[source * group + part]
        for row in range(9):
            pieces_of[row].append([rows[9 * g + row : 9 * g + row + 1] for g in range(whole)])
            if width % PAIR:
                at = 9 * whole + row % 4 if row < 8 else 9 * whole + 4
                tail = rows[at : at + 1, NA:] if 4 <= row < 8 else rows[at : at + 1, :NA]
                pieces_of[row][-1].append(tail)
    factor = jnp.concatenate(factors, axis=0)
    for row in range(9):
        for index in range(len(pieces_of[row][0])):
            value = jnp.concatenate([of_replica[index] for of_replica in pieces_of[row]], axis=0)
            size = value.shape[1]
            if row == 2:
                lane = lax.broadcasted_iota(jnp.int32, value.shape, 1)
                value = value - (domain * (width // NA) + (index * PAIR + lane) // NA).astype(jnp.float32)
            elif row // 3 == 1:
                value = value * factor[:, :size]
            outs[row // 3][row % 3, :, index * PAIR : index * PAIR + size] = value


VMEM_SPEC = pl.BlockSpec(memory_space=pltpu.VMEM)
SMEM_SPEC = pl.BlockSpec(memory_space=pltpu.SMEM)


def run_prepare(place, state, features, per_replica, weights, small):
    atoms, channels = features.shape
    own_pairs = atoms // per_replica // PAIR
    extended = own_pairs + 2
    return pl.pallas_call(
        prepare,
        out_shape=(
            jax.ShapeDtypeStruct((extended, 8, PAIR), jnp.float32),
            jax.ShapeDtypeStruct((own_pairs, 8, PAIR), jnp.float32),
            jax.ShapeDtypeStruct((extended * PAIR, channels), jnp.bfloat16),
            jax.ShapeDtypeStruct((extended * PAIR, channels), jnp.bfloat16),
            jax.ShapeDtypeStruct(((extended - 1) * PAIR, channels), jnp.float32),
            jax.ShapeDtypeStruct((8, channels), jnp.float32),
        ),
        in_specs=[SMEM_SPEC] + [VMEM_SPEC] * 4,
        out_specs=(VMEM_SPEC,) * 6,
        compiler_params=pltpu.CompilerParams(vmem_limit_bytes=20 * 1024 * 1024),
    )(place, state, features, weights, small)


def run_advance(stage, parts_count, last_shape, x, v, g, edge, got, own_feat, table, message_push, later_push, weights, small):
    own_pairs = v.shape[0]
    channels = table.shape[1]
    basis_count = small.shape[0] - SMALL_ROWS
    tiles = jax.ShapeDtypeStruct(v.shape, jnp.float32)
    lhs = pltpu.VMEM(((basis_count + 3) * NA, PAIR), jnp.bfloat16)
    vec = pltpu.VMEM((3 * NA, PAIR), jnp.bfloat16)
    message = pltpu.VMEM((PAIR, 2 * channels), jnp.bfloat16)
    return pl.pallas_call(
        functools.partial(advance, stage, parts_count),
        out_shape=(tiles, tiles, tiles, jax.ShapeDtypeStruct(last_shape, jnp.float32)),
        in_specs=[VMEM_SPEC] * 11,
        out_specs=(VMEM_SPEC,) * 4,
        scratch_shapes=[
            pltpu.VMEM((own_pairs + 2, 8, PAIR), jnp.float32),
            pltpu.VMEM((own_pairs + 1, 8, PAIR), jnp.float32),
            [[lhs] * 3] * 2,
            [[vec] * 3] * 2,
            message,
            message,
            pltpu.VMEM((own_pairs + 2, 3, 8, PAIR), jnp.float32),
        ],
        compiler_params=pltpu.CompilerParams(vmem_limit_bytes=20 * 1024 * 1024),
    )(x, v, g, edge, got, own_feat, table, message_push, later_push, weights, small)


def run_steps(place, state, features, per_replica, chunk_shape, exchange, weights, small):
    x, v, *fixed = run_prepare(place, state, features, per_replica, weights, small)
    edge_shape = (2, 2, 8, PAIR)
    edge = got = jnp.zeros(edge_shape, jnp.float32)
    g = v
    for step in range(STEPS + 1):
        stage = min(step, 2) if step < STEPS else 3
        shape = edge_shape if step < STEPS else chunk_shape
        x, v, g, edge = run_advance(stage, per_replica, shape, x, v, g, edge, got, *fixed, weights, small)
        if step < STEPS:
            got = exchange(edge)
    return edge


def run_finish(place, source, got, thermal_targets, local_atoms):
    replicas = thermal_targets.shape[0]
    out = jax.ShapeDtypeStruct((3, replicas, local_atoms), jnp.float32)
    whole = pl.BlockSpec(out.shape, lambda: (0, 0, 0))
    outs = pl.pallas_call(
        finish,
        out_shape=(out, out, out),
        in_specs=[SMEM_SPEC, SMEM_SPEC, VMEM_SPEC, SMEM_SPEC],
        out_specs=(whole, whole, whole),
    )(place, source, got, thermal_targets)
    return tuple(jnp.transpose(o, (1, 0, 2)) for o in outs)


def on_device(
    particle_places,
    particle_speeds,
    thermal_targets,
    element_features,
    swap_counterpart_slot,
    swap_approval_flags,
    initial_signal_projector,
    initial_distance_filter,
    initial_directional_scales,
    invariant_revision_matrix,
    magnitude_revision_matrix,
    later_signal_projector,
    later_directional_scales,
    push_output_matrix,
):
    replicas = particle_places.shape[0]
    local_atoms = particle_places.shape[2]
    local_cells = local_atoms // NA
    devices = lax.axis_size("dom")
    own = lax.axis_index("dom")
    per_replica = devices // replicas
    bits = devices.bit_length() - 1
    replica_bits = replicas.bit_length() - 1

    def trade(value, mask):
        return lax.ppermute(value, "dom", [(i, i ^ mask) for i in range(devices)])

    weights = jnp.concatenate(
        [initial_signal_projector, invariant_revision_matrix, magnitude_revision_matrix, later_signal_projector], axis=0
    )
    span = initial_distance_filter.shape[0] - 1
    order = (jnp.arange(span + 1, dtype=jnp.float32) - 0.5 * span)[:, None]
    channels = element_features.shape[1]
    part = own % per_replica
    cells = float(devices * local_cells)
    thermal = lax.dynamic_slice(thermal_targets, (own // per_replica,), (1,))
    small = jnp.concatenate(
        [
            initial_distance_filter * jnp.exp(-2.0 * order * order),
            (initial_directional_scales * initial_directional_scales)[None],
            (push_output_matrix * initial_directional_scales)[None],
            (push_output_matrix * later_directional_scales)[None],
            jnp.broadcast_to(thermal[:, None], (1, channels)),
            jnp.broadcast_to(jnp.where(part == 0, -cells, 0.0), (1, channels)),
            jnp.broadcast_to(jnp.where(part == per_replica - 1, cells, 0.0), (1, channels)),
            jnp.broadcast_to(part.astype(jnp.float32), (1, channels)),
        ],
        axis=0,
    )
    place = jnp.stack([part, jnp.full((), per_replica, own.dtype), own]).astype(jnp.int32)
    ladder_slot = jnp.arange(replicas, dtype=jnp.int32)
    source = jnp.where(swap_approval_flags > 0, swap_counterpart_slot, ladder_slot)

    atom_cell = jnp.arange(local_atoms, dtype=jnp.int32) // NA
    cell_floor = jnp.array([0.0, 0.0, 1.0], jnp.float32)[:, None] * (
        own * local_cells + atom_cell
    ).astype(jnp.float32)
    state = jnp.concatenate([particle_places - cell_floor, particle_speeds], axis=1)
    upper_part = lax.reduce_precision(state, 8, 7)
    state = jnp.stack([upper_part, state - upper_part], axis=1).astype(jnp.bfloat16)
    channels = element_features.shape[1]
    state = state.reshape(replicas, -1, channels)
    state_rows = state.shape[1]
    features = element_features
    for level in range(bits):
        mask = devices >> (level + 1)
        upper = (own & mask) > 0
        if level < replica_bits:
            half = state.shape[0] // 2
            keep = jnp.where(upper, state[half:], state[:half])
            send = jnp.where(upper, state[:half], state[half:])
        else:
            keep = send = state
        message = jnp.concatenate([features.reshape(-1, channels), send.reshape(-1, channels)], axis=0)
        if level == 1:
            message, weights, small, place, source = lax.optimization_barrier((message, weights, small, place, source))
        got = trade(message, mask)
        count = features.size // channels
        got_features = got[:count].reshape(features.shape)
        got = got[count:].reshape(send.shape)
        axis = 1 + level
        state = jnp.stack([jnp.where(upper, got, keep), jnp.where(upper, keep, got)], axis=axis)
        features = jnp.stack(
            [jnp.where(upper, got_features, features), jnp.where(upper, features, got_features)], axis=level
        )
    state = state.reshape(devices, 2, 6, local_atoms).astype(jnp.float32)
    state = (state[:, 0] + state[:, 1]).transpose(1, 0, 2).reshape(6, devices * local_atoms)
    features = features.reshape(devices * local_atoms, -1)

    def exchange(edge):
        if per_replica == 2:
            return trade(edge, 1)
        groups = [list(range(i, i + per_replica)) for i in range(0, devices, per_replica)]
        up = [(a, b) for g in groups for a, b in zip(g, g[1:] + g[:1])]
        kinetic = lax.psum(edge[0, 1, 3], "dom", axis_index_groups=groups) - edge[0, 1, 3]
        before = lax.ppermute(edge[1], "dom", up)
        after = lax.ppermute(edge[0], "dom", [(b, a) for a, b in up])
        return jnp.stack([after.at[1, 3].set(kinetic), before])

    chunk_rows = 9 * (local_atoms // PAIR) + (5 if local_atoms % PAIR else 0) + 1
    chunk_rows = -(-chunk_rows // 8) * 8
    chunks = run_steps(place, state, features, per_replica, (devices, chunk_rows, PAIR), exchange, weights, small)
    got = lax.all_to_all(chunks, "dom", 0, 0)
    return run_finish(place, source, got, thermal_targets, local_atoms)


def solution(mesh):
    return jax.shard_map(
        on_device,
        mesh=mesh,
        in_specs=(
            P("groups", None, "dom"),
            P("groups", None, "dom"),
            P("groups"),
            P(("groups", "dom"), None),
            P("groups"),
            P("groups"),
            P(),
            P(),
            P(),
            P(),
            P(),
            P(),
            P(),
            P(),
        ),
        out_specs=(P("groups", None, "dom"), P("groups", None, "dom"), P("groups", None, "dom")),
        check_vma=False,
    )
```

```python
import functools
import math

import jax
import jax.numpy as jnp
from jax import lax
from jax.experimental import pallas as pl
from jax.experimental.pallas import tpu as pltpu
from jax.sharding import PartitionSpec as P

NA = 64
PAIR = 2 * NA
STEPS = 4
UNROLL = 2
SMALL_ROWS = 7
CHUNK = 16
CHUNKS = NA // CHUNK

step_time = 0.05
motion_work_lower_limit = 1e-06
LOG2E = math.log2(math.e)
VMEM_SPEC = pl.BlockSpec(memory_space=pltpu.VMEM)


def dot(a, b):
    return jnp.dot(a, b, preferred_element_type=jnp.float32)


def dot_rows(a, b):
    return lax.dot_general(a, b, (((1,), (1,)), ((), ())), preferred_element_type=jnp.float32)


def pieces(value, count):
    width = value.shape[1]
    row = lax.broadcasted_iota(jnp.int32, (16, width), 0)
    tile = jnp.zeros((16, width), jnp.float32)
    for index in range(count):
        part = value.astype(jnp.bfloat16).astype(jnp.float32)
        tile = jnp.where(row == index, part, tile)
        value = value - part
    return tile.astype(jnp.bfloat16)


def swap_halves(first, second):
    low = lax.broadcasted_iota(jnp.int32, first.shape, first.ndim - 1) < NA
    return pltpu.roll(jnp.where(low, second, first), NA, first.ndim - 1)


def basis(displacement, basis_count):
    dx, dy, dz = displacement
    rest = jnp.maximum(1.0 - (dx * dx + dy * dy + dz * dz), 0.0)
    envelope = rest * rest
    vectors = [dx * envelope, dy * envelope, dz * envelope]
    span = basis_count - 1
    rate = 2.0 * span * LOG2E
    offset = 0.5 - rest
    center = jnp.exp2((-2.0 * span * span * LOG2E) * (offset * offset)) * envelope
    slope = rate * offset
    up = jnp.exp2(slope)
    down = jnp.exp2(-slope)
    up_two = up * up
    down_two = down * down
    rising = [center * up]
    falling = [center * down]
    for _ in range(basis_count // 2 - 1):
        rising.append(rising[-1] * up_two)
        falling.append(falling[-1] * down_two)
    return falling[::-1] + rising, vectors


def prepare(
    parts_count,
    state_ref,
    feat_ref,
    weight_ref,
    small_ref,
    x_out,
    v_out,
    own_feat,
    table,
    message_push,
    later_push,
):
    extended = x_out.shape[0]
    cells = feat_ref.shape[0] // NA
    own_cells = 2 * (extended - 2)
    part = lax.rem(lax.axis_index("dom"), parts_count)
    first_cell = part * own_cells - 2 + cells
    for p in range(extended):
        cell = lax.rem(first_cell + 2 * p, cells)
        at = pl.ds(pl.multiple_of(cell * NA, PAIR), PAIR)
        rows = state_ref[:, at]
        x = jnp.concatenate([rows[:3], jnp.zeros((5, PAIR), jnp.float32)], axis=0)
        sub = lax.broadcasted_iota(jnp.int32, (8, PAIR), 0)
        lane = lax.broadcasted_iota(jnp.int32, (8, PAIR), 1)
        floor = (part * own_cells - 2 + 2 * p + lane // NA).astype(jnp.float32)
        x_out[p] = x + jnp.where(sub == 2, floor, 0.0)
        if 0 < p < extended - 1:
            v_out[p - 1] = jnp.concatenate([rows[3:6], jnp.zeros((5, PAIR), jnp.float32)], axis=0)
        own_feat[p * PAIR : (p + 1) * PAIR, :] = feat_ref[at, :]
    channels = feat_ref.shape[1]
    basis_count = small_ref.shape[0] - SMALL_ROWS
    table[...] = dot(own_feat[...], weight_ref[:channels, :]).astype(jnp.bfloat16)
    message_push[...] = (
        table[NA : NA + (extended - 1) * PAIR, :].astype(jnp.float32) * small_ref[basis_count + 1 : basis_count + 2, :]
    )
    parts = dot_rows(pieces(small_ref[basis_count + 2 : basis_count + 3, :], 3), weight_ref[3 * channels :, :])
    later_push[...] = jnp.broadcast_to(jnp.sum(parts, axis=0, keepdims=True), later_push.shape)


def advance(
    stage,
    parts_count,
    x_ref,
    v_ref,
    g_ref,
    edge_ref,
    got_ref,
    own_feat,
    table,
    message_push,
    later_push,
    weight_ref,
    small_ref,
    x_out,
    v_out,
    g_out,
    last_out,
    e_rows,
    h_rows,
    lhs,
    vec,
    message_0,
    message_1,
    forces,
):
    own_pairs = v_ref.shape[0]
    extended = own_pairs + 2
    pairs = own_pairs + 1
    total_cells = float(2 * own_pairs * parts_count)
    channels = small_ref.shape[1]
    basis_count = small_ref.shape[0] - SMALL_ROWS
    sub = lax.broadcasted_iota(jnp.int32, (8, PAIR), 0)
    low = lax.broadcasted_iota(jnp.int32, (1, PAIR), 1) < NA
    filters = small_ref[:basis_count, :]
    filters = jnp.concatenate([filters, filters], axis=1)
    scale_square = small_ref[basis_count : basis_count + 1, :]
    scale_square = jnp.concatenate([scale_square, scale_square], axis=1)

    if stage == 0:
        e_rows[...] = x_ref[...]
        half_v = v_ref[...]
    else:
        if stage == 1:
            stretch = jnp.ones((1, 1), jnp.float32)
        else:
            kinetic = edge_ref[0, 1, 3:4, 0:1] + got_ref[0, 1, 3:4, 0:1]
            mean = kinetic / (3.0 * NA * total_cells) + motion_work_lower_limit
            stretch = jnp.sqrt(small_ref[basis_count + 3 : basis_count + 4, 0:1] / mean)
        v = v_ref[...] * stretch
        half_v = v + (0.5 * step_time) * g_ref[...]
        e_rows[1 : own_pairs + 1] = x_ref[...] + step_time * v
        z_only = jnp.where(sub == 2, 1.0, 0.0)
        left = got_ref[1, 0] + (step_time * stretch) * got_ref[1, 1]
        right = got_ref[0, 0] + (step_time * stretch) * got_ref[0, 1]
        e_rows[0] = left + z_only * small_ref[basis_count + 4 : basis_count + 5, :]
        e_rows[extended - 1] = right + z_only * small_ref[basis_count + 5 : basis_count + 6, :]
    h_rows[...] = swap_halves(e_rows[0:pairs], e_rows[1:extended])

    blank = jnp.zeros((PAIR, channels), jnp.bfloat16)
    def beside(value):
        return jnp.concatenate([value, jnp.zeros_like(value)], axis=1)

    message = (message_0, message_1)

    def make_rows(q, chunk, columns, out):
        before = e_rows[q]
        after = e_rows[q + 1]
        across = jnp.where(low, after, before)
        start = chunk * CHUNK
        own_a = [columns[start : start + CHUNK, c : c + 1] for c in range(3)]
        own_b = [columns[NA + start : NA + start + CHUNK, c : c + 1] for c in range(3)]
        own_a = [jnp.broadcast_to(o, (CHUNK, PAIR)) for o in own_a]
        own_b = [jnp.broadcast_to(o, (CHUNK, PAIR)) for o in own_b]
        blocks = (
            [before[c : c + 1] - own_a[c] for c in range(3)],
            [after[c : c + 1] - own_b[c] for c in range(3)],
            [across[c : c + 1] - jnp.where(low, own_a[c], own_b[c]) for c in range(3)],
        )
        for block, displacement in enumerate(blocks):
            radials, vectors = basis(displacement, basis_count)
            for k, value in enumerate(radials + vectors):
                out[block][k * NA + start : k * NA + start + CHUNK, :] = value.astype(jnp.bfloat16)

    def make_messages(q, rows, out):
        if isinstance(q, int):
            near = table[q * PAIR : (q + 2) * PAIR, :]
        else:
            near = table[pl.ds(pl.multiple_of(q * PAIR, PAIR), 2 * PAIR), :]
        across = jnp.concatenate(
            [
                jnp.concatenate([near[PAIR : 3 * NA], blank[:NA]], axis=1),
                jnp.concatenate([blank[:NA], near[NA:PAIR]], axis=1),
            ],
            axis=0,
        )
        shared = dot(rows[2][...], across)
        for own in range(2):
            at = slice(own * channels, (own + 1) * channels)
            total = dot(rows[own][...], near[own * PAIR : (own + 1) * PAIR]) + shared[:, at]
            total = [total[k * NA : (k + 1) * NA] for k in range(basis_count + 3)]
            scalar = total[0] * filters[0:1, :channels]
            for k in range(1, basis_count):
                scalar = scalar + total[k] * filters[k : k + 1, :channels]
            norm = total[basis_count] * total[basis_count]
            for k in range(basis_count + 1, basis_count + 3):
                norm = norm + total[k] * total[k]
            out[own * NA : (own + 1) * NA, :channels] = scalar.astype(jnp.bfloat16)
            out[own * NA : (own + 1) * NA, channels:] = (norm * scale_square[:, :channels]).astype(jnp.bfloat16)

    def make_pull(q, message_ref):
        if isinstance(q, int):
            at_feat = slice(NA + q * PAIR, NA + (q + 1) * PAIR)
            at_push = slice(q * PAIR, (q + 1) * PAIR)
        else:
            at_feat = pl.ds(pl.multiple_of(q * PAIR, PAIR) + NA, PAIR)
            at_push = pl.ds(pl.multiple_of(q * PAIR, PAIR), PAIR)
        half = 0.5 * dot(message_ref[...], weight_ref[channels : 3 * channels, :])
        hidden = (own_feat[at_feat, :].astype(jnp.float32) + (half + half * jnp.tanh(half))).astype(jnp.bfloat16)
        pull = hidden.astype(jnp.float32) * later_push[0:1] + message_push[at_push, :]
        return jnp.sum(pull, axis=1, keepdims=True)

    def make_force(q, c, pull, blocks):
        first = jnp.broadcast_to(pull[:NA], (NA, PAIR))
        second = jnp.broadcast_to(pull[NA:], (NA, PAIR))
        weights = (first, second, jnp.where(low, first, second))
        totals = []
        for ref, weight in zip(blocks, weights):
            value = ref[c * NA : (c + 1) * NA, :].astype(jnp.float32) * weight
            total = value[:8]
            for row in range(8, NA, 8):
                total = total + value[row : row + 8]
            totals.append(total)
        forces[q, c] = forces[q, c] - totals[0] - jnp.where(low, 0.0, totals[2])
        forces[q + 1, c] = -totals[1] - jnp.where(low, totals[2], 0.0)

    forces[0] = jnp.zeros(forces.shape[1:], jnp.float32)

    def stage_of(q, t, rows=True, before=True):
        here, there = t % 2, (t + 1) % 2
        if before:
            pull = make_pull(q - 1, message[there])
            for c in range(3):
                make_force(q - 1, c, pull, vec[there])
        make_messages(q, lhs[here], message[here])
        for block in range(3):
            vec[here][block][...] = lhs[here][block][basis_count * NA :, :]
        if rows:
            columns = jnp.transpose(h_rows[q + 1])
            for chunk in range(CHUNKS):
                make_rows(q + 1, chunk, columns, lhs[there])

    columns = jnp.transpose(h_rows[0])
    for chunk in range(CHUNKS):
        make_rows(0, chunk, columns, lhs[0])
    whole = (pairs - 2) // UNROLL
    stage_of(0, 0, before=False)

    def several(i, _):
        for t in range(UNROLL):
            stage_of(i * UNROLL + t + 1, t + 1)
        return 0

    lax.fori_loop(0, whole, several, 0)
    for q in range(whole * UNROLL + 1, pairs):
        stage_of(q, q, rows=q < pairs - 1)
    last = pairs - 1
    pull = make_pull(last, message[last % 2])
    for c in range(3):
        make_force(last, c, pull, vec[last % 2])

    for p in range(own_pairs):
        tile = jnp.zeros((8, PAIR), jnp.float32)
        for c in range(3):
            tile = jnp.where(sub == c, jnp.sum(forces[p + 1, c], axis=0, keepdims=True), tile)
        g_out[p] = tile
    g = g_out[...]
    if stage == 0:
        v = half_v
    else:
        v = half_v + (0.5 * step_time) * g
    v_out[...] = v
    kinetic = jnp.sum(v * v, axis=0)
    kinetic = jnp.sum(jnp.sum(kinetic, axis=1, keepdims=True), axis=0, keepdims=True)
    x = e_rows[1 : own_pairs + 1]
    if stage < 3:
        x_out[...] = x + (0.5 * step_time * step_time) * g
        for edge, p in enumerate((0, own_pairs - 1)):
            last_out[edge, 0] = x_out[p]
            last_out[edge, 1] = jnp.where(sub == 3, kinetic, v[p])
        return
    x_out[...] = x
    rows = jnp.concatenate(
        [
            jnp.concatenate([x_out[p, 0:3], v_out[p, 0:3], g_out[p, 0:3]], axis=0)
            for p in range(own_pairs)
        ],
        axis=1,
    )
    chunks = last_out.shape[0] // parts_count
    width = own_pairs * PAIR // chunks
    whole = width // PAIR
    last_out[...] = jnp.zeros(last_out.shape, jnp.float32)
    end = last_out.shape[1] - 1
    last_out[:, end:, :] = jnp.broadcast_to(kinetic.reshape(1, 1, 1), (last_out.shape[0], 1, PAIR))
    part = small_ref[basis_count + 6 : basis_count + 7, :]
    for chunk in range(parts_count * chunks):
        chosen = part == float(chunk // chunks)
        at = chunk % chunks * width
        for group in range(whole):
            last_out[chunk, 9 * group : 9 * (group + 1), :] = jnp.where(chosen, rows[:, at : at + PAIR], 0.0)
            at = at + PAIR
        if width % PAIR:
            tail = jnp.where(chosen[:, :NA], rows[:, at : at + NA], 0.0)
            last_out[chunk, 9 * whole : 9 * whole + 4, :] = jnp.concatenate([tail[:4], tail[4:8]], axis=1)
            last_out[chunk, 9 * whole + 4 : 9 * whole + 5, :NA] = tail[8:]


def finish(ladder_ref, got_ref, x_out, v_out, g_out):
    replicas, width = x_out.shape[1:]
    whole = width // PAIR
    domains, chunk_rows = got_ref.shape[:2]
    group = domains // replicas
    domain = lax.axis_index("dom")
    part = domain // (domains // group)
    atoms = float(domains * width)
    outs = (x_out, v_out, g_out)
    pieces_of = [[] for _ in range(9)]
    factors = []
    sources = [got_ref[s * group + part] for s in range(replicas)]
    kinetics = []
    for s in range(replicas):
        kinetic = got_ref[s * group, chunk_rows - 1 :, :]
        for other in range(1, group):
            kinetic = kinetic + got_ref[s * group + other, chunk_rows - 1 :, :]
        kinetics.append(kinetic)
    targets = [jnp.broadcast_to(ladder_ref[0:1, r : r + 1], (1, PAIR)) for r in range(replicas)]
    source_targets = []
    for r in range(replicas):
        own_source = jnp.broadcast_to(ladder_ref[1:2, r : r + 1], (1, PAIR))
        rows, kinetic, source_target = sources[0], kinetics[0], targets[0]
        for s in range(1, replicas):
            chosen = own_source == float(s)
            rows = jnp.where(chosen, sources[s], rows)
            kinetic = jnp.where(chosen, kinetics[s], kinetic)
            source_target = jnp.where(chosen, targets[s], source_target)
        source_targets.append(source_target)
        factors.append(kinetic)
        for row in range(9):
            pieces_of[row].append([rows[9 * g + row : 9 * g + row + 1] for g in range(whole)])
            if width % PAIR:
                at = 9 * whole + row % 4 if row < 8 else 9 * whole + 4
                tail = rows[at : at + 1, NA:] if 4 <= row < 8 else rows[at : at + 1, :NA]
                pieces_of[row][-1].append(tail)
    mean = jnp.concatenate(factors, axis=0) / (3.0 * atoms) + motion_work_lower_limit
    source_target = jnp.concatenate(source_targets, axis=0)
    target = jnp.concatenate(targets, axis=0)
    factor = jnp.sqrt(source_target / mean) * jnp.sqrt(target / source_target)
    for row in range(9):
        for index in range(len(pieces_of[row][0])):
            value = jnp.concatenate([of_replica[index] for of_replica in pieces_of[row]], axis=0)
            size = value.shape[1]
            if row == 2:
                lane = lax.broadcasted_iota(jnp.int32, value.shape, 1)
                value = value - (domain * (width // NA) + (index * PAIR + lane) // NA).astype(jnp.float32)
            elif row // 3 == 1:
                value = value * factor[:, :size]
            outs[row // 3][row % 3, :, index * PAIR : index * PAIR + size] = value


def run_prepare(state, features, per_replica, weights, small):
    atoms, channels = features.shape
    own_pairs = atoms // per_replica // PAIR
    extended = own_pairs + 2
    return pl.pallas_call(
        functools.partial(prepare, per_replica),
        out_shape=(
            jax.ShapeDtypeStruct((extended, 8, PAIR), jnp.float32),
            jax.ShapeDtypeStruct((own_pairs, 8, PAIR), jnp.float32),
            jax.ShapeDtypeStruct((extended * PAIR, channels), jnp.bfloat16),
            jax.ShapeDtypeStruct((extended * PAIR, channels), jnp.bfloat16),
            jax.ShapeDtypeStruct(((extended - 1) * PAIR, channels), jnp.float32),
            jax.ShapeDtypeStruct((8, channels), jnp.float32),
        ),
        in_specs=[VMEM_SPEC] * 4,
        out_specs=(VMEM_SPEC,) * 6,
        compiler_params=pltpu.CompilerParams(vmem_limit_bytes=20 * 1024 * 1024),
    )(state, features, weights, small)


def run_advance(stage, parts_count, last_shape, x, v, g, edge, got, own_feat, table, message_push, later_push, weights, small):
    own_pairs = v.shape[0]
    channels = table.shape[1]
    basis_count = small.shape[0] - SMALL_ROWS
    tiles = jax.ShapeDtypeStruct(v.shape, jnp.float32)
    lhs = pltpu.VMEM(((basis_count + 3) * NA, PAIR), jnp.bfloat16)
    vec = pltpu.VMEM((3 * NA, PAIR), jnp.bfloat16)
    message = pltpu.VMEM((PAIR, 2 * channels), jnp.bfloat16)
    return pl.pallas_call(
        functools.partial(advance, stage, parts_count),
        out_shape=(tiles, tiles, tiles, jax.ShapeDtypeStruct(last_shape, jnp.float32)),
        in_specs=[VMEM_SPEC] * 11,
        out_specs=(VMEM_SPEC,) * 4,
        scratch_shapes=[
            pltpu.VMEM((own_pairs + 2, 8, PAIR), jnp.float32),
            pltpu.VMEM((own_pairs + 1, 8, PAIR), jnp.float32),
            [[lhs] * 3] * 2,
            [[vec] * 3] * 2,
            message,
            message,
            pltpu.VMEM((own_pairs + 2, 3, 8, PAIR), jnp.float32),
        ],
        compiler_params=pltpu.CompilerParams(vmem_limit_bytes=20 * 1024 * 1024),
    )(x, v, g, edge, got, own_feat, table, message_push, later_push, weights, small)


def run_steps(state, features, per_replica, chunk_shape, exchange, weights, small):
    x, v, *fixed = run_prepare(state, features, per_replica, weights, small)
    edge_shape = (2, 2, 8, PAIR)
    edge = got = jnp.zeros(edge_shape, jnp.float32)
    g = v
    for step in range(STEPS + 1):
        stage = min(step, 2) if step < STEPS else 3
        shape = edge_shape if step < STEPS else chunk_shape
        x, v, g, edge = run_advance(stage, per_replica, shape, x, v, g, edge, got, *fixed, weights, small)
        if step < STEPS:
            got = exchange(edge)
    return edge


def run_finish(ladder, got, local_atoms):
    replicas = ladder.shape[1]
    out = jax.ShapeDtypeStruct((3, replicas, local_atoms), jnp.float32)
    whole = pl.BlockSpec(out.shape, lambda: (0, 0, 0))
    outs = pl.pallas_call(
        finish,
        out_shape=(out, out, out),
        in_specs=[VMEM_SPEC] * 2,
        out_specs=(whole, whole, whole),
        compiler_params=pltpu.CompilerParams(vmem_limit_bytes=8 * 1024 * 1024),
    )(ladder, got)
    return tuple(jnp.transpose(o, (1, 0, 2)) for o in outs)


def on_device(
    particle_places,
    particle_speeds,
    thermal_targets,
    element_features,
    swap_counterpart_slot,
    swap_approval_flags,
    initial_signal_projector,
    initial_distance_filter,
    initial_directional_scales,
    invariant_revision_matrix,
    magnitude_revision_matrix,
    later_signal_projector,
    later_directional_scales,
    push_output_matrix,
):
    replicas = particle_places.shape[0]
    local_atoms = particle_places.shape[2]
    local_cells = local_atoms // NA
    devices = lax.axis_size("dom")
    own = lax.axis_index("dom")
    per_replica = devices // replicas
    bits = devices.bit_length() - 1
    replica_bits = replicas.bit_length() - 1

    def trade(value, mask):
        return lax.ppermute(value, "dom", [(i, i ^ mask) for i in range(devices)])

    weights = jnp.concatenate(
        [initial_signal_projector, invariant_revision_matrix, magnitude_revision_matrix, later_signal_projector], axis=0
    )
    span = initial_distance_filter.shape[0] - 1
    order = (jnp.arange(span + 1, dtype=jnp.float32) - 0.5 * span)[:, None]
    channels = element_features.shape[1]
    part = own % per_replica
    cells = float(devices * local_cells)
    thermal = lax.dynamic_slice(thermal_targets, (own // per_replica,), (1,))
    small = jnp.concatenate(
        [
            initial_distance_filter * jnp.exp(-2.0 * order * order),
            (initial_directional_scales * initial_directional_scales)[None],
            (push_output_matrix * initial_directional_scales)[None],
            (push_output_matrix * later_directional_scales)[None],
            jnp.broadcast_to(thermal[:, None], (1, channels)),
            jnp.broadcast_to(jnp.where(part == 0, -cells, 0.0), (1, channels)),
            jnp.broadcast_to(jnp.where(part == per_replica - 1, cells, 0.0), (1, channels)),
            jnp.broadcast_to(part.astype(jnp.float32), (1, channels)),
        ],
        axis=0,
    )

    slots = jnp.arange(replicas, dtype=jnp.int32)
    source = jnp.where(swap_approval_flags > 0, swap_counterpart_slot, slots)
    ladder = jnp.stack([thermal_targets, source.astype(jnp.float32)])

    atom_cell = jnp.arange(local_atoms, dtype=jnp.int32) // NA
    cell_floor = jnp.array([0.0, 0.0, 1.0], jnp.float32)[:, None] * (
        own * local_cells + atom_cell
    ).astype(jnp.float32)
    state = jnp.concatenate([particle_places - cell_floor, particle_speeds], axis=1)
    upper_part = lax.reduce_precision(state, 8, 7)
    state = jnp.stack([upper_part, state - upper_part], axis=1).astype(jnp.bfloat16)
    channels = element_features.shape[1]
    state = state.reshape(replicas, -1, channels)
    state_rows = state.shape[1]
    features = element_features
    for level in range(bits):
        mask = devices >> (level + 1)
        upper = (own & mask) > 0
        if level < replica_bits:
            half = state.shape[0] // 2
            keep = jnp.where(upper, state[half:], state[:half])
            send = jnp.where(upper, state[:half], state[half:])
        else:
            keep = send = state
        message = jnp.concatenate([features.reshape(-1, channels), send.reshape(-1, channels)], axis=0)
        if level == 1:
            message, weights, small, ladder = lax.optimization_barrier((message, weights, small, ladder))
        got = trade(message, mask)
        count = features.size // channels
        got_features = got[:count].reshape(features.shape)
        got = got[count:].reshape(send.shape)
        axis = 1 + level
        state = jnp.stack([jnp.where(upper, got, keep), jnp.where(upper, keep, got)], axis=axis)
        features = jnp.stack(
            [jnp.where(upper, got_features, features), jnp.where(upper, features, got_features)], axis=level
        )
    state = state.reshape(devices, 2, 6, local_atoms).astype(jnp.float32)
    state = (state[:, 0] + state[:, 1]).transpose(1, 0, 2).reshape(6, devices * local_atoms)
    features = features.reshape(devices * local_atoms, -1)

    def exchange(edge):
        if per_replica == 2:
            return trade(edge, 1)
        groups = [list(range(i, i + per_replica)) for i in range(0, devices, per_replica)]
        up = [(a, b) for g in groups for a, b in zip(g, g[1:] + g[:1])]
        kinetic = lax.psum(edge[0, 1, 3], "dom", axis_index_groups=groups) - edge[0, 1, 3]
        before = lax.ppermute(edge[1], "dom", up)
        after = lax.ppermute(edge[0], "dom", [(b, a) for a, b in up])
        return jnp.stack([after.at[1, 3].set(kinetic), before])

    chunk_rows = 9 * (local_atoms // PAIR) + (5 if local_atoms % PAIR else 0) + 1
    chunk_rows = -(-chunk_rows // 8) * 8
    chunks = run_steps(state, features, per_replica, (devices, chunk_rows, PAIR), exchange, weights, small)
    got = lax.all_to_all(chunks, "dom", 0, 0)
    return run_finish(ladder, got, local_atoms)


def solution(mesh):
    return jax.shard_map(
        on_device,
        mesh=mesh,
        in_specs=(
            P("groups", None, "dom"),
            P("groups", None, "dom"),
            P("groups"),
            P(("groups", "dom"), None),
            P("groups"),
            P("groups"),
            P(),
            P(),
            P(),
            P(),
            P(),
            P(),
            P(),
            P(),
        ),
        out_specs=(P("groups", None, "dom"), P("groups", None, "dom"), P("groups", None, "dom")),
        check_vma=False,
    )
```

```python
import functools
import math

import jax
import jax.numpy as jnp
from jax import lax
from jax.experimental import pallas as pl
from jax.experimental.pallas import tpu as pltpu
from jax.sharding import PartitionSpec as P

NA = 64
PAIR = 2 * NA
STEPS = 4
UNROLL = 2
SMALL_ROWS = 7
CHUNK = 16
CHUNKS = NA // CHUNK

step_time = 0.05
motion_work_lower_limit = 1e-06
LOG2E = math.log2(math.e)
STEP_INPUTS = 11
VMEM_SPEC = pl.BlockSpec(memory_space=pltpu.VMEM)


def dot(a, b):
    return jnp.dot(a, b, preferred_element_type=jnp.float32)


def dot_rows(a, b):
    return lax.dot_general(a, b, (((1,), (1,)), ((), ())), preferred_element_type=jnp.float32)


def pieces(value, count):
    width = value.shape[1]
    row = lax.broadcasted_iota(jnp.int32, (16, width), 0)
    tile = jnp.zeros((16, width), jnp.float32)
    for index in range(count):
        part = value.astype(jnp.bfloat16).astype(jnp.float32)
        tile = jnp.where(row == index, part, tile)
        value = value - part
    return tile.astype(jnp.bfloat16)


def swap_halves(first, second):
    low = lax.broadcasted_iota(jnp.int32, first.shape, first.ndim - 1) < NA
    return pltpu.roll(jnp.where(low, second, first), NA, first.ndim - 1)


def basis(displacement, basis_count):
    dx, dy, dz = displacement
    rest = jnp.maximum(1.0 - (dx * dx + dy * dy + dz * dz), 0.0)
    envelope = rest * rest
    vectors = [dx * envelope, dy * envelope, dz * envelope]
    span = basis_count - 1
    rate = 2.0 * span * LOG2E
    offset = 0.5 - rest
    center = jnp.exp2((-2.0 * span * span * LOG2E) * (offset * offset)) * envelope
    slope = rate * offset
    up = jnp.exp2(slope)
    down = jnp.exp2(-slope)
    up_two = up * up
    down_two = down * down
    rising = [center * up]
    falling = [center * down]
    for _ in range(basis_count // 2 - 1):
        rising.append(rising[-1] * up_two)
        falling.append(falling[-1] * down_two)
    return falling[::-1] + rising, vectors


def prepare(
    parts_count,
    state_ref,
    feat_ref,
    weight_ref,
    small_ref,
    x_out,
    v_out,
    own_feat,
    table,
    message_push,
    later_push,
):
    extended = x_out.shape[0]
    cells = feat_ref.shape[0] // NA
    own_cells = 2 * (extended - 2)
    part = lax.rem(lax.axis_index("dom"), parts_count)
    first_cell = part * own_cells - 2 + cells
    for p in range(extended):
        cell = lax.rem(first_cell + 2 * p, cells)
        at = pl.ds(pl.multiple_of(cell * NA, PAIR), PAIR)
        rows = state_ref[:, at]
        x = jnp.concatenate([rows[:3], jnp.zeros((5, PAIR), jnp.float32)], axis=0)
        sub = lax.broadcasted_iota(jnp.int32, (8, PAIR), 0)
        lane = lax.broadcasted_iota(jnp.int32, (8, PAIR), 1)
        floor = (part * own_cells - 2 + 2 * p + lane // NA).astype(jnp.float32)
        x_out[p] = x + jnp.where(sub == 2, floor, 0.0)
        if 0 < p < extended - 1:
            v_out[p - 1] = jnp.concatenate([rows[3:6], jnp.zeros((5, PAIR), jnp.float32)], axis=0)
        own_feat[p * PAIR : (p + 1) * PAIR, :] = feat_ref[at, :]
    channels = feat_ref.shape[1]
    basis_count = small_ref.shape[0] - SMALL_ROWS
    table[...] = dot(own_feat[...], weight_ref[:channels, :]).astype(jnp.bfloat16)
    message_push[...] = (
        table[NA : NA + (extended - 1) * PAIR, :].astype(jnp.float32) * small_ref[basis_count + 1 : basis_count + 2, :]
    )
    parts = dot_rows(pieces(small_ref[basis_count + 2 : basis_count + 3, :], 3), weight_ref[3 * channels :, :])
    later_push[...] = jnp.broadcast_to(jnp.sum(parts, axis=0, keepdims=True), later_push.shape)


def advance(
    stage,
    parts_count,
    x_ref,
    v_ref,
    g_ref,
    edge_ref,
    got_ref,
    own_feat,
    table,
    message_push,
    later_push,
    weight_ref,
    small_ref,
    x_out,
    v_out,
    g_out,
    last_out,
    e_rows,
    h_rows,
    lhs,
    vec,
    message_0,
    message_1,
    forces,
):
    own_pairs = v_ref.shape[0]
    extended = own_pairs + 2
    pairs = own_pairs + 1
    total_cells = float(2 * own_pairs * parts_count)
    channels = small_ref.shape[1]
    basis_count = small_ref.shape[0] - SMALL_ROWS
    sub = lax.broadcasted_iota(jnp.int32, (8, PAIR), 0)
    low = lax.broadcasted_iota(jnp.int32, (1, PAIR), 1) < NA
    filters = small_ref[:basis_count, :]
    filters = jnp.concatenate([filters, filters], axis=1)
    scale_square = small_ref[basis_count : basis_count + 1, :]
    scale_square = jnp.concatenate([scale_square, scale_square], axis=1)

    if stage == 0:
        e_rows[...] = x_ref[...]
        half_v = v_ref[...]
    else:
        if stage == 1:
            stretch = jnp.ones((1, 1), jnp.float32)
        else:
            kinetic = edge_ref[0, 1, 3:4, 0:1] + got_ref[0, 1, 3:4, 0:1]
            mean = kinetic / (3.0 * NA * total_cells) + motion_work_lower_limit
            stretch = jnp.sqrt(small_ref[basis_count + 3 : basis_count + 4, 0:1] / mean)
        v = v_ref[...] * stretch
        half_v = v + (0.5 * step_time) * g_ref[...]
        e_rows[1 : own_pairs + 1] = x_ref[...] + step_time * v
        z_only = jnp.where(sub == 2, 1.0, 0.0)
        left = got_ref[1, 0] + (step_time * stretch) * got_ref[1, 1]
        right = got_ref[0, 0] + (step_time * stretch) * got_ref[0, 1]
        e_rows[0] = left + z_only * small_ref[basis_count + 4 : basis_count + 5, :]
        e_rows[extended - 1] = right + z_only * small_ref[basis_count + 5 : basis_count + 6, :]
    h_rows[...] = swap_halves(e_rows[0:pairs], e_rows[1:extended])

    blank = jnp.zeros((PAIR, channels), jnp.bfloat16)
    def beside(value):
        return jnp.concatenate([value, jnp.zeros_like(value)], axis=1)

    message = (message_0, message_1)

    def make_rows(q, chunk, columns, out):
        before = e_rows[q]
        after = e_rows[q + 1]
        across = jnp.where(low, after, before)
        start = chunk * CHUNK
        own_a = [columns[start : start + CHUNK, c : c + 1] for c in range(3)]
        own_b = [columns[NA + start : NA + start + CHUNK, c : c + 1] for c in range(3)]
        own_a = [jnp.broadcast_to(o, (CHUNK, PAIR)) for o in own_a]
        own_b = [jnp.broadcast_to(o, (CHUNK, PAIR)) for o in own_b]
        blocks = (
            [before[c : c + 1] - own_a[c] for c in range(3)],
            [after[c : c + 1] - own_b[c] for c in range(3)],
            [across[c : c + 1] - jnp.where(low, own_a[c], own_b[c]) for c in range(3)],
        )
        for block, displacement in enumerate(blocks):
            radials, vectors = basis(displacement, basis_count)
            for k, value in enumerate(radials + vectors):
                out[block][k * NA + start : k * NA + start + CHUNK, :] = value.astype(jnp.bfloat16)

    def make_messages(q, rows, out):
        if isinstance(q, int):
            near = table[q * PAIR : (q + 2) * PAIR, :]
        else:
            near = table[pl.ds(pl.multiple_of(q * PAIR, PAIR), 2 * PAIR), :]
        across = jnp.concatenate(
            [
                jnp.concatenate([near[PAIR : 3 * NA], blank[:NA]], axis=1),
                jnp.concatenate([blank[:NA], near[NA:PAIR]], axis=1),
            ],
            axis=0,
        )
        shared = dot(rows[2][...], across)
        for own in range(2):
            at = slice(own * channels, (own + 1) * channels)
            total = dot(rows[own][...], near[own * PAIR : (own + 1) * PAIR]) + shared[:, at]
            total = [total[k * NA : (k + 1) * NA] for k in range(basis_count + 3)]
            scalar = total[0] * filters[0:1, :channels]
            for k in range(1, basis_count):
                scalar = scalar + total[k] * filters[k : k + 1, :channels]
            norm = total[basis_count] * total[basis_count]
            for k in range(basis_count + 1, basis_count + 3):
                norm = norm + total[k] * total[k]
            out[own * NA : (own + 1) * NA, :channels] = scalar.astype(jnp.bfloat16)
            out[own * NA : (own + 1) * NA, channels:] = (norm * scale_square[:, :channels]).astype(jnp.bfloat16)

    def make_pull(q, message_ref):
        if isinstance(q, int):
            at_feat = slice(NA + q * PAIR, NA + (q + 1) * PAIR)
            at_push = slice(q * PAIR, (q + 1) * PAIR)
        else:
            at_feat = pl.ds(pl.multiple_of(q * PAIR, PAIR) + NA, PAIR)
            at_push = pl.ds(pl.multiple_of(q * PAIR, PAIR), PAIR)
        half = 0.5 * dot(message_ref[...], weight_ref[channels : 3 * channels, :])
        hidden = (own_feat[at_feat, :].astype(jnp.float32) + (half + half * jnp.tanh(half))).astype(jnp.bfloat16)
        pull = hidden.astype(jnp.float32) * later_push[0:1] + message_push[at_push, :]
        return jnp.sum(pull, axis=1, keepdims=True)

    def make_force(q, c, pull, blocks):
        first = jnp.broadcast_to(pull[:NA], (NA, PAIR))
        second = jnp.broadcast_to(pull[NA:], (NA, PAIR))
        weights = (first, second, jnp.where(low, first, second))
        totals = []
        for ref, weight in zip(blocks, weights):
            value = ref[c * NA : (c + 1) * NA, :].astype(jnp.float32) * weight
            total = value[:8]
            for row in range(8, NA, 8):
                total = total + value[row : row + 8]
            totals.append(total)
        forces[q, c] = forces[q, c] - totals[0] - jnp.where(low, 0.0, totals[2])
        forces[q + 1, c] = -totals[1] - jnp.where(low, totals[2], 0.0)

    forces[0] = jnp.zeros(forces.shape[1:], jnp.float32)

    def stage_of(q, t, rows=True, before=True):
        here, there = t % 2, (t + 1) % 2
        if before:
            pull = make_pull(q - 1, message[there])
            for c in range(3):
                make_force(q - 1, c, pull, vec[there])
        make_messages(q, lhs[here], message[here])
        for block in range(3):
            vec[here][block][...] = lhs[here][block][basis_count * NA :, :]
        if rows:
            columns = jnp.transpose(h_rows[q + 1])
            for chunk in range(CHUNKS):
                make_rows(q + 1, chunk, columns, lhs[there])

    columns = jnp.transpose(h_rows[0])
    for chunk in range(CHUNKS):
        make_rows(0, chunk, columns, lhs[0])
    whole = (pairs - 2) // UNROLL
    stage_of(0, 0, before=False)

    def several(i, _):
        for t in range(UNROLL):
            stage_of(i * UNROLL + t + 1, t + 1)
        return 0

    lax.fori_loop(0, whole, several, 0)
    for q in range(whole * UNROLL + 1, pairs):
        stage_of(q, q, rows=q < pairs - 1)
    last = pairs - 1
    pull = make_pull(last, message[last % 2])
    for c in range(3):
        make_force(last, c, pull, vec[last % 2])

    for p in range(own_pairs):
        tile = jnp.zeros((8, PAIR), jnp.float32)
        for c in range(3):
            tile = jnp.where(sub == c, jnp.sum(forces[p + 1, c], axis=0, keepdims=True), tile)
        g_out[p] = tile
    g = g_out[...]
    if stage == 0:
        v = half_v
    else:
        v = half_v + (0.5 * step_time) * g
    v_out[...] = v
    kinetic = jnp.sum(v * v, axis=0)
    kinetic = jnp.sum(jnp.sum(kinetic, axis=1, keepdims=True), axis=0, keepdims=True)
    x = e_rows[1 : own_pairs + 1]
    if stage < 3:
        x_out[...] = x + (0.5 * step_time * step_time) * g
        for edge, p in enumerate((0, own_pairs - 1)):
            last_out[edge, 0] = x_out[p]
            last_out[edge, 1] = jnp.where(sub == 3, kinetic, v[p])
        return
    x_out[...] = x
    rows = jnp.concatenate(
        [
            jnp.concatenate([x_out[p, 0:3], v_out[p, 0:3], g_out[p, 0:3]], axis=0)
            for p in range(own_pairs)
        ],
        axis=1,
    )
    chunks = last_out.shape[0] // parts_count
    width = own_pairs * PAIR // chunks
    whole = width // PAIR
    last_out[...] = jnp.zeros(last_out.shape, jnp.float32)
    end = last_out.shape[1] - 1
    last_out[:, end:, :] = jnp.broadcast_to(kinetic.reshape(1, 1, 1), (last_out.shape[0], 1, PAIR))
    part = small_ref[basis_count + 6 : basis_count + 7, :]
    for chunk in range(parts_count * chunks):
        chosen = part == float(chunk // chunks)
        at = chunk % chunks * width
        for group in range(whole):
            last_out[chunk, 9 * group : 9 * (group + 1), :] = jnp.where(chosen, rows[:, at : at + PAIR], 0.0)
            at = at + PAIR
        if width % PAIR:
            tail = jnp.where(chosen[:, :NA], rows[:, at : at + NA], 0.0)
            last_out[chunk, 9 * whole : 9 * whole + 4, :] = jnp.concatenate([tail[:4], tail[4:8]], axis=1)
            last_out[chunk, 9 * whole + 4 : 9 * whole + 5, :NA] = tail[8:]


def finish(ladder_ref, got_ref, x_out, v_out, g_out):
    replicas, width = x_out.shape[1:]
    whole = width // PAIR
    domains, chunk_rows = got_ref.shape[:2]
    group = domains // replicas
    domain = lax.axis_index("dom")
    part = domain // (domains // group)
    atoms = float(domains * width)
    outs = (x_out, v_out, g_out)
    pieces_of = [[] for _ in range(9)]
    factors = []
    sources = [got_ref[s * group + part] for s in range(replicas)]
    kinetics = []
    for s in range(replicas):
        kinetic = got_ref[s * group, chunk_rows - 1 :, :]
        for other in range(1, group):
            kinetic = kinetic + got_ref[s * group + other, chunk_rows - 1 :, :]
        kinetics.append(kinetic)
    targets = [jnp.broadcast_to(ladder_ref[0:1, r : r + 1], (1, PAIR)) for r in range(replicas)]
    source_targets = []
    for r in range(replicas):
        own_source = jnp.broadcast_to(ladder_ref[1:2, r : r + 1], (1, PAIR))
        rows, kinetic, source_target = sources[0], kinetics[0], targets[0]
        for s in range(1, replicas):
            chosen = own_source == float(s)
            rows = jnp.where(chosen, sources[s], rows)
            kinetic = jnp.where(chosen, kinetics[s], kinetic)
            source_target = jnp.where(chosen, targets[s], source_target)
        source_targets.append(source_target)
        factors.append(kinetic)
        for row in range(9):
            pieces_of[row].append([rows[9 * g + row : 9 * g + row + 1] for g in range(whole)])
            if width % PAIR:
                at = 9 * whole + row % 4 if row < 8 else 9 * whole + 4
                tail = rows[at : at + 1, NA:] if 4 <= row < 8 else rows[at : at + 1, :NA]
                pieces_of[row][-1].append(tail)
    mean = jnp.concatenate(factors, axis=0) / (3.0 * atoms) + motion_work_lower_limit
    source_target = jnp.concatenate(source_targets, axis=0)
    target = jnp.concatenate(targets, axis=0)
    factor = jnp.sqrt(source_target / mean) * jnp.sqrt(target / source_target)
    for row in range(9):
        for index in range(len(pieces_of[row][0])):
            value = jnp.concatenate([of_replica[index] for of_replica in pieces_of[row]], axis=0)
            size = value.shape[1]
            if row == 2:
                lane = lax.broadcasted_iota(jnp.int32, value.shape, 1)
                value = value - (domain * (width // NA) + (index * PAIR + lane) // NA).astype(jnp.float32)
            elif row // 3 == 1:
                value = value * factor[:, :size]
            outs[row // 3][row % 3, :, index * PAIR : index * PAIR + size] = value


def run_prepare(state, features, per_replica, weights, small):
    atoms, channels = features.shape
    own_pairs = atoms // per_replica // PAIR
    extended = own_pairs + 2
    return pl.pallas_call(
        functools.partial(prepare, per_replica),
        out_shape=(
            jax.ShapeDtypeStruct((extended, 8, PAIR), jnp.float32),
            jax.ShapeDtypeStruct((own_pairs, 8, PAIR), jnp.float32),
            jax.ShapeDtypeStruct((extended * PAIR, channels), jnp.bfloat16),
            jax.ShapeDtypeStruct((extended * PAIR, channels), jnp.bfloat16),
            jax.ShapeDtypeStruct(((extended - 1) * PAIR, channels), jnp.float32),
            jax.ShapeDtypeStruct((8, channels), jnp.float32),
        ),
        in_specs=[VMEM_SPEC] * 4,
        out_specs=(VMEM_SPEC,) * 6,
        compiler_params=pltpu.CompilerParams(vmem_limit_bytes=20 * 1024 * 1024),
    )(state, features, weights, small)


def advance_last(stage, parts_count, *refs):
    inputs, last, state, rest = refs[:STEP_INPUTS], refs[STEP_INPUTS], refs[STEP_INPUTS + 1 :][:3], refs[STEP_INPUTS + 4 :]
    advance(stage, parts_count, *inputs, *state, last, *rest)


def run_advance(stage, parts_count, last_shape, x, v, g, edge, got, own_feat, table, message_push, later_push, weights, small):
    own_pairs = v.shape[0]
    channels = table.shape[1]
    basis_count = small.shape[0] - SMALL_ROWS
    tiles = jax.ShapeDtypeStruct(v.shape, jnp.float32)
    lhs = pltpu.VMEM(((basis_count + 3) * NA, PAIR), jnp.bfloat16)
    vec = pltpu.VMEM((3 * NA, PAIR), jnp.bfloat16)
    message = pltpu.VMEM((PAIR, 2 * channels), jnp.bfloat16)
    last = stage == 3
    state = [] if last else [tiles] * 3
    outs = pl.pallas_call(
        functools.partial(advance_last if last else advance, stage, parts_count),
        out_shape=(*state, jax.ShapeDtypeStruct(last_shape, jnp.float32)),
        in_specs=[VMEM_SPEC] * STEP_INPUTS,
        out_specs=(VMEM_SPEC,) * (len(state) + 1),
        scratch_shapes=([pltpu.VMEM(v.shape, jnp.float32)] * 3 if last else [])
        + [
            pltpu.VMEM((own_pairs + 2, 8, PAIR), jnp.float32),
            pltpu.VMEM((own_pairs + 1, 8, PAIR), jnp.float32),
            [[lhs] * 3] * 2,
            [[vec] * 3] * 2,
            message,
            message,
            pltpu.VMEM((own_pairs + 2, 3, 8, PAIR), jnp.float32),
        ],
        compiler_params=pltpu.CompilerParams(vmem_limit_bytes=20 * 1024 * 1024),
    )(x, v, g, edge, got, own_feat, table, message_push, later_push, weights, small)
    return (None, None, None, *outs) if last else outs


def run_steps(state, features, per_replica, chunk_shape, exchange, weights, small):
    x, v, *fixed = run_prepare(state, features, per_replica, weights, small)
    edge_shape = (2, 2, 8, PAIR)
    edge = got = jnp.zeros(edge_shape, jnp.float32)
    g = v
    for step in range(STEPS + 1):
        stage = min(step, 2) if step < STEPS else 3
        shape = edge_shape if step < STEPS else chunk_shape
        x, v, g, edge = run_advance(stage, per_replica, shape, x, v, g, edge, got, *fixed, weights, small)
        if step < STEPS:
            got = exchange(edge)
    return edge


def run_finish(ladder, got, local_atoms):
    replicas = ladder.shape[1]
    out = jax.ShapeDtypeStruct((3, replicas, local_atoms), jnp.float32)
    whole = pl.BlockSpec(out.shape, lambda: (0, 0, 0))
    outs = pl.pallas_call(
        finish,
        out_shape=(out, out, out),
        in_specs=[VMEM_SPEC] * 2,
        out_specs=(whole, whole, whole),
        compiler_params=pltpu.CompilerParams(vmem_limit_bytes=8 * 1024 * 1024),
    )(ladder, got)
    return tuple(jnp.transpose(o, (1, 0, 2)) for o in outs)


def on_device(
    particle_places,
    particle_speeds,
    thermal_targets,
    element_features,
    swap_counterpart_slot,
    swap_approval_flags,
    initial_signal_projector,
    initial_distance_filter,
    initial_directional_scales,
    invariant_revision_matrix,
    magnitude_revision_matrix,
    later_signal_projector,
    later_directional_scales,
    push_output_matrix,
):
    replicas = particle_places.shape[0]
    local_atoms = particle_places.shape[2]
    local_cells = local_atoms // NA
    devices = lax.axis_size("dom")
    own = lax.axis_index("dom")
    per_replica = devices // replicas
    bits = devices.bit_length() - 1
    replica_bits = replicas.bit_length() - 1

    def trade(value, mask):
        return lax.ppermute(value, "dom", [(i, i ^ mask) for i in range(devices)])

    weights = jnp.concatenate(
        [initial_signal_projector, invariant_revision_matrix, magnitude_revision_matrix, later_signal_projector], axis=0
    )
    span = initial_distance_filter.shape[0] - 1
    order = (jnp.arange(span + 1, dtype=jnp.float32) - 0.5 * span)[:, None]
    channels = element_features.shape[1]
    part = own % per_replica
    cells = float(devices * local_cells)
    thermal = lax.dynamic_slice(thermal_targets, (own // per_replica,), (1,))
    small = jnp.concatenate(
        [
            initial_distance_filter * jnp.exp(-2.0 * order * order),
            (initial_directional_scales * initial_directional_scales)[None],
            (push_output_matrix * initial_directional_scales)[None],
            (push_output_matrix * later_directional_scales)[None],
            jnp.broadcast_to(thermal[:, None], (1, channels)),
            jnp.broadcast_to(jnp.where(part == 0, -cells, 0.0), (1, channels)),
            jnp.broadcast_to(jnp.where(part == per_replica - 1, cells, 0.0), (1, channels)),
            jnp.broadcast_to(part.astype(jnp.float32), (1, channels)),
        ],
        axis=0,
    )

    slots = jnp.arange(replicas, dtype=jnp.int32)
    source = jnp.where(swap_approval_flags > 0, swap_counterpart_slot, slots)
    ladder = jnp.stack([thermal_targets, source.astype(jnp.float32)])

    atom_cell = jnp.arange(local_atoms, dtype=jnp.int32) // NA
    cell_floor = jnp.array([0.0, 0.0, 1.0], jnp.float32)[:, None] * (
        own * local_cells + atom_cell
    ).astype(jnp.float32)
    state = jnp.concatenate([particle_places - cell_floor, particle_speeds], axis=1)
    upper_part = lax.reduce_precision(state, 8, 7)
    state = jnp.stack([upper_part, state - upper_part], axis=1).astype(jnp.bfloat16)
    channels = element_features.shape[1]
    state = state.reshape(replicas, -1, channels)
    state_rows = state.shape[1]
    features = element_features
    for level in range(bits):
        mask = devices >> (level + 1)
        upper = (own & mask) > 0
        if level < replica_bits:
            half = state.shape[0] // 2
            keep = jnp.where(upper, state[half:], state[:half])
            send = jnp.where(upper, state[:half], state[half:])
        else:
            keep = send = state
        message = jnp.concatenate([features.reshape(-1, channels), send.reshape(-1, channels)], axis=0)
        if level == 1:
            message, weights, small, ladder = lax.optimization_barrier((message, weights, small, ladder))
        got = trade(message, mask)
        count = features.size // channels
        got_features = got[:count].reshape(features.shape)
        got = got[count:].reshape(send.shape)
        axis = 1 + level
        state = jnp.stack([jnp.where(upper, got, keep), jnp.where(upper, keep, got)], axis=axis)
        features = jnp.stack(
            [jnp.where(upper, got_features, features), jnp.where(upper, features, got_features)], axis=level
        )
    state = state.reshape(devices, 2, 6, local_atoms).astype(jnp.float32)
    state = (state[:, 0] + state[:, 1]).transpose(1, 0, 2).reshape(6, devices * local_atoms)
    features = features.reshape(devices * local_atoms, -1)

    def exchange(edge):
        if per_replica == 2:
            return trade(edge, 1)
        groups = [list(range(i, i + per_replica)) for i in range(0, devices, per_replica)]
        up = [(a, b) for g in groups for a, b in zip(g, g[1:] + g[:1])]
        kinetic = lax.psum(edge[0, 1, 3], "dom", axis_index_groups=groups) - edge[0, 1, 3]
        before = lax.ppermute(edge[1], "dom", up)
        after = lax.ppermute(edge[0], "dom", [(b, a) for a, b in up])
        return jnp.stack([after.at[1, 3].set(kinetic), before])

    chunk_rows = 9 * (local_atoms // PAIR) + (5 if local_atoms % PAIR else 0) + 1
    chunk_rows = -(-chunk_rows // 8) * 8
    chunks = run_steps(state, features, per_replica, (devices, chunk_rows, PAIR), exchange, weights, small)
    got = lax.all_to_all(chunks, "dom", 0, 0)
    return run_finish(ladder, got, local_atoms)


def solution(mesh):
    return jax.shard_map(
        on_device,
        mesh=mesh,
        in_specs=(
            P("groups", None, "dom"),
            P("groups", None, "dom"),
            P("groups"),
            P(("groups", "dom"), None),
            P("groups"),
            P("groups"),
            P(),
            P(),
            P(),
            P(),
            P(),
            P(),
            P(),
            P(),
        ),
        out_specs=(P("groups", None, "dom"), P("groups", None, "dom"), P("groups", None, "dom")),
        check_vma=False,
    )
```

```python
import functools
import math

import jax
import jax.numpy as jnp
from jax import lax
from jax.experimental import pallas as pl
from jax.experimental.pallas import tpu as pltpu
from jax.sharding import PartitionSpec as P

NA = 64
PAIR = 2 * NA
STEPS = 4
UNROLL = 2
SMALL_ROWS = 7
CHUNK = 16
CHUNKS = NA // CHUNK

step_time = 0.05
motion_work_lower_limit = 1e-06
LOG2E = math.log2(math.e)
STEP_INPUTS = 11
VMEM_SPEC = pl.BlockSpec(memory_space=pltpu.VMEM)


def dot(a, b):
    return jnp.dot(a, b, preferred_element_type=jnp.float32)


def dot_rows(a, b):
    return lax.dot_general(a, b, (((1,), (1,)), ((), ())), preferred_element_type=jnp.float32)


def pieces(value, count):
    width = value.shape[1]
    row = lax.broadcasted_iota(jnp.int32, (16, width), 0)
    tile = jnp.zeros((16, width), jnp.float32)
    for index in range(count):
        part = value.astype(jnp.bfloat16).astype(jnp.float32)
        tile = jnp.where(row == index, part, tile)
        value = value - part
    return tile.astype(jnp.bfloat16)


def swap_halves(first, second):
    low = lax.broadcasted_iota(jnp.int32, first.shape, first.ndim - 1) < NA
    return pltpu.roll(jnp.where(low, second, first), NA, first.ndim - 1)


def basis(displacement, basis_count):
    dx, dy, dz = displacement
    rest = jnp.maximum(1.0 - (dx * dx + dy * dy + dz * dz), 0.0)
    envelope = rest * rest
    vectors = [dx * envelope, dy * envelope, dz * envelope]
    span = basis_count - 1
    rate = 2.0 * span * LOG2E
    offset = 0.5 - rest
    center = jnp.exp2((-2.0 * span * span * LOG2E) * (offset * offset)) * envelope
    slope = rate * offset
    up = jnp.exp2(slope)
    down = jnp.exp2(-slope)
    up_two = up * up
    down_two = down * down
    rising = [center * up]
    falling = [center * down]
    for _ in range(basis_count // 2 - 1):
        rising.append(rising[-1] * up_two)
        falling.append(falling[-1] * down_two)
    return falling[::-1] + rising, vectors


def prepare(
    parts_count,
    state_ref,
    feat_ref,
    weight_ref,
    small_ref,
    x_out,
    v_out,
    own_feat,
    table,
    message_push,
    later_push,
):
    extended = x_out.shape[0]
    cells = feat_ref.shape[0] // NA
    own_cells = 2 * (extended - 2)
    part = lax.rem(lax.axis_index("dom"), parts_count)
    first_cell = part * own_cells - 2 + cells
    for p in range(extended):
        cell = lax.rem(first_cell + 2 * p, cells)
        at = pl.ds(pl.multiple_of(cell * NA, PAIR), PAIR)
        rows = state_ref[:, at]
        x = jnp.concatenate([rows[:3], jnp.zeros((5, PAIR), jnp.float32)], axis=0)
        sub = lax.broadcasted_iota(jnp.int32, (8, PAIR), 0)
        lane = lax.broadcasted_iota(jnp.int32, (8, PAIR), 1)
        floor = (part * own_cells - 2 + 2 * p + lane // NA).astype(jnp.float32)
        x_out[p] = x + jnp.where(sub == 2, floor, 0.0)
        if 0 < p < extended - 1:
            v_out[p - 1] = jnp.concatenate([rows[3:6], jnp.zeros((5, PAIR), jnp.float32)], axis=0)
        own_feat[p * PAIR : (p + 1) * PAIR, :] = feat_ref[at, :]
    channels = feat_ref.shape[1]
    basis_count = small_ref.shape[0] - SMALL_ROWS
    table[...] = dot(own_feat[...], weight_ref[:channels, :]).astype(jnp.bfloat16)
    message_push[...] = (
        table[NA : NA + (extended - 1) * PAIR, :].astype(jnp.float32) * small_ref[basis_count + 1 : basis_count + 2, :]
    )
    parts = dot_rows(pieces(small_ref[basis_count + 2 : basis_count + 3, :], 3), weight_ref[3 * channels :, :])
    later_push[...] = jnp.broadcast_to(jnp.sum(parts, axis=0, keepdims=True), later_push.shape)


def advance(
    stage,
    parts_count,
    x_ref,
    v_ref,
    g_ref,
    edge_ref,
    got_ref,
    own_feat,
    table,
    message_push,
    later_push,
    weight_ref,
    small_ref,
    x_out,
    v_out,
    g_out,
    last_out,
    e_rows,
    h_rows,
    lhs,
    vec,
    message_0,
    message_1,
    forces,
):
    own_pairs = v_ref.shape[0]
    extended = own_pairs + 2
    pairs = own_pairs + 1
    total_cells = float(2 * own_pairs * parts_count)
    channels = small_ref.shape[1]
    basis_count = small_ref.shape[0] - SMALL_ROWS
    sub = lax.broadcasted_iota(jnp.int32, (8, PAIR), 0)
    low = lax.broadcasted_iota(jnp.int32, (1, PAIR), 1) < NA
    filters = small_ref[:basis_count, :]
    filters = jnp.concatenate([filters, filters], axis=1)
    scale_square = small_ref[basis_count : basis_count + 1, :]
    scale_square = jnp.concatenate([scale_square, scale_square], axis=1)

    if stage == 0:
        e_rows[...] = x_ref[...]
        half_v = v_ref[...]
    else:
        if stage == 1:
            stretch = jnp.ones((1, 1), jnp.float32)
        else:
            kinetic = edge_ref[0, 1, 3:4, 0:1] + got_ref[0, 1, 3:4, 0:1]
            mean = kinetic / (3.0 * NA * total_cells) + motion_work_lower_limit
            stretch = jnp.sqrt(small_ref[basis_count + 3 : basis_count + 4, 0:1] / mean)
        v = v_ref[...] * stretch
        half_v = v + (0.5 * step_time) * g_ref[...]
        e_rows[1 : own_pairs + 1] = x_ref[...] + step_time * v
        z_only = jnp.where(sub == 2, 1.0, 0.0)
        left = got_ref[1, 0] + (step_time * stretch) * got_ref[1, 1]
        right = got_ref[0, 0] + (step_time * stretch) * got_ref[0, 1]
        e_rows[0] = left + z_only * small_ref[basis_count + 4 : basis_count + 5, :]
        e_rows[extended - 1] = right + z_only * small_ref[basis_count + 5 : basis_count + 6, :]
    h_rows[...] = swap_halves(e_rows[0:pairs], e_rows[1:extended])

    blank = jnp.zeros((PAIR, channels), jnp.bfloat16)
    def beside(value):
        return jnp.concatenate([value, jnp.zeros_like(value)], axis=1)

    message = (message_0, message_1)

    def make_rows(q, chunk, columns, out):
        before = e_rows[q]
        after = e_rows[q + 1]
        across = jnp.where(low, after, before)
        start = chunk * CHUNK
        own_a = [columns[start : start + CHUNK, c : c + 1] for c in range(3)]
        own_b = [columns[NA + start : NA + start + CHUNK, c : c + 1] for c in range(3)]
        own_a = [jnp.broadcast_to(o, (CHUNK, PAIR)) for o in own_a]
        own_b = [jnp.broadcast_to(o, (CHUNK, PAIR)) for o in own_b]
        blocks = (
            [before[c : c + 1] - own_a[c] for c in range(3)],
            [after[c : c + 1] - own_b[c] for c in range(3)],
            [across[c : c + 1] - jnp.where(low, own_a[c], own_b[c]) for c in range(3)],
        )
        for block, displacement in enumerate(blocks):
            radials, vectors = basis(displacement, basis_count)
            for k, value in enumerate(radials + vectors):
                out[block][k * NA + start : k * NA + start + CHUNK, :] = value.astype(jnp.bfloat16)

    def make_messages(q, rows, out):
        if isinstance(q, int):
            near = table[q * PAIR : (q + 2) * PAIR, :]
        else:
            near = table[pl.ds(pl.multiple_of(q * PAIR, PAIR), 2 * PAIR), :]
        across = jnp.concatenate(
            [
                jnp.concatenate([near[PAIR : 3 * NA], blank[:NA]], axis=1),
                jnp.concatenate([blank[:NA], near[NA:PAIR]], axis=1),
            ],
            axis=0,
        )
        shared = dot(rows[2][...], across)
        for own in range(2):
            at = slice(own * channels, (own + 1) * channels)
            total = dot(rows[own][...], near[own * PAIR : (own + 1) * PAIR]) + shared[:, at]
            total = [total[k * NA : (k + 1) * NA] for k in range(basis_count + 3)]
            scalar = total[0] * filters[0:1, :channels]
            for k in range(1, basis_count):
                scalar = scalar + total[k] * filters[k : k + 1, :channels]
            norm = total[basis_count] * total[basis_count]
            for k in range(basis_count + 1, basis_count + 3):
                norm = norm + total[k] * total[k]
            out[own * NA : (own + 1) * NA, :channels] = scalar.astype(jnp.bfloat16)
            out[own * NA : (own + 1) * NA, channels:] = (norm * scale_square[:, :channels]).astype(jnp.bfloat16)

    def make_pull(q, message_ref):
        if isinstance(q, int):
            at_feat = slice(NA + q * PAIR, NA + (q + 1) * PAIR)
            at_push = slice(q * PAIR, (q + 1) * PAIR)
        else:
            at_feat = pl.ds(pl.multiple_of(q * PAIR, PAIR) + NA, PAIR)
            at_push = pl.ds(pl.multiple_of(q * PAIR, PAIR), PAIR)
        half = 0.5 * dot(message_ref[...], weight_ref[channels : 3 * channels, :])
        hidden = (own_feat[at_feat, :].astype(jnp.float32) + (half + half * jnp.tanh(half))).astype(jnp.bfloat16)
        pull = hidden.astype(jnp.float32) * later_push[0:1] + message_push[at_push, :]
        return jnp.sum(pull, axis=1, keepdims=True)

    def make_force(q, c, pull, blocks):
        first = jnp.broadcast_to(pull[:NA], (NA, PAIR))
        second = jnp.broadcast_to(pull[NA:], (NA, PAIR))
        weights = (first, second, jnp.where(low, first, second))
        totals = []
        for ref, weight in zip(blocks, weights):
            value = ref[c * NA : (c + 1) * NA, :].astype(jnp.float32) * weight
            total = value[:8]
            for row in range(8, NA, 8):
                total = total + value[row : row + 8]
            totals.append(total)
        forces[q, c] = forces[q, c] - totals[0] - jnp.where(low, 0.0, totals[2])
        forces[q + 1, c] = -totals[1] - jnp.where(low, totals[2], 0.0)

    forces[0] = jnp.zeros(forces.shape[1:], jnp.float32)

    def stage_of(q, t, rows=True, before=True):
        here, there = t % 2, (t + 1) % 2
        if before:
            pull = make_pull(q - 1, message[there])
            for c in range(3):
                make_force(q - 1, c, pull, vec[there])
        make_messages(q, lhs[here], message[here])
        for block in range(3):
            vec[here][block][...] = lhs[here][block][basis_count * NA :, :]
        if rows:
            columns = jnp.transpose(h_rows[q + 1])
            for chunk in range(CHUNKS):
                make_rows(q + 1, chunk, columns, lhs[there])

    columns = jnp.transpose(h_rows[0])
    for chunk in range(CHUNKS):
        make_rows(0, chunk, columns, lhs[0])
    whole = (pairs - 2) // UNROLL
    stage_of(0, 0, before=False)

    def several(i, _):
        for t in range(UNROLL):
            stage_of(i * UNROLL + t + 1, t + 1)
        return 0

    lax.fori_loop(0, whole, several, 0)
    for q in range(whole * UNROLL + 1, pairs):
        stage_of(q, q, rows=q < pairs - 1)
    last = pairs - 1
    pull = make_pull(last, message[last % 2])
    for c in range(3):
        make_force(last, c, pull, vec[last % 2])

    for p in range(own_pairs):
        tile = jnp.zeros((8, PAIR), jnp.float32)
        for c in range(3):
            tile = jnp.where(sub == c, jnp.sum(forces[p + 1, c], axis=0, keepdims=True), tile)
        g_out[p] = tile
    g = g_out[...]
    if stage == 0:
        v = half_v
    else:
        v = half_v + (0.5 * step_time) * g
    v_out[...] = v
    kinetic = jnp.sum(v * v, axis=0)
    kinetic = jnp.sum(jnp.sum(kinetic, axis=1, keepdims=True), axis=0, keepdims=True)
    x = e_rows[1 : own_pairs + 1]
    if stage < 3:
        x_out[...] = x + (0.5 * step_time * step_time) * g
        for edge, p in enumerate((0, own_pairs - 1)):
            last_out[edge, 0] = x_out[p]
            last_out[edge, 1] = jnp.where(sub == 3, kinetic, v[p])
        return
    x_out[...] = x
    part = small_ref[basis_count + 6 : basis_count + 7, :]
    for p in range(own_pairs):
        floor = part * float(2 * own_pairs) + float(2 * p) + jnp.where(low, 0.0, 1.0)
        x_out[p] = x_out[p] - jnp.where(sub == 2, floor, 0.0)
    kinetic_high = kinetic.astype(jnp.bfloat16).astype(jnp.float32)
    kinetic = jnp.where(low, kinetic_high, kinetic - kinetic_high)
    rows = jnp.concatenate(
        [
            jnp.concatenate([x_out[p, 0:3], v_out[p, 0:3], g_out[p, 0:3]], axis=0)
            for p in range(own_pairs)
        ],
        axis=1,
    )
    chunks = last_out.shape[0] // parts_count
    width = own_pairs * PAIR // chunks
    whole = width // PAIR
    last_out[...] = jnp.zeros(last_out.shape, jnp.float32)
    end = last_out.shape[1] - 1
    last_out[:, end:, :] = jnp.broadcast_to(kinetic.reshape(1, 1, PAIR), (last_out.shape[0], 1, PAIR))
    for chunk in range(parts_count * chunks):
        chosen = part == float(chunk // chunks)
        at = chunk % chunks * width
        for group in range(whole):
            last_out[chunk, 9 * group : 9 * (group + 1), :] = jnp.where(chosen, rows[:, at : at + PAIR], 0.0)
            at = at + PAIR
        if width % PAIR:
            tail = jnp.where(chosen[:, :NA], rows[:, at : at + NA], 0.0)
            last_out[chunk, 9 * whole : 9 * whole + 4, :] = jnp.concatenate([tail[:4], tail[4:8]], axis=1)
            last_out[chunk, 9 * whole + 4 : 9 * whole + 5, :NA] = tail[8:]


def finish(ladder_ref, got_ref, x_out, v_out, g_out):
    replicas, width = x_out.shape[1:]
    whole = width // PAIR
    domains, chunk_rows = got_ref.shape[:2]
    group = domains // replicas
    domain = lax.axis_index("dom")
    part = domain // (domains // group)
    atoms = float(domains * width)
    outs = (x_out, v_out, g_out)
    pieces_of = [[] for _ in range(9)]
    factors = []
    sources = [got_ref[s * group + part].astype(jnp.float32) for s in range(replicas)]
    kinetics = []
    for s in range(replicas):
        kinetic = got_ref[s * group].astype(jnp.float32)[chunk_rows - 1 :]
        for other in range(1, group):
            kinetic = kinetic + got_ref[s * group + other].astype(jnp.float32)[chunk_rows - 1 :]
        kinetics.append(kinetic + pltpu.roll(kinetic, NA, 1))
    targets = [jnp.broadcast_to(ladder_ref[0:1, r : r + 1], (1, PAIR)) for r in range(replicas)]
    source_targets = []
    for r in range(replicas):
        own_source = jnp.broadcast_to(ladder_ref[1:2, r : r + 1], (1, PAIR))
        rows, kinetic, source_target = sources[0], kinetics[0], targets[0]
        for s in range(1, replicas):
            chosen = own_source == float(s)
            rows = jnp.where(chosen, sources[s], rows)
            kinetic = jnp.where(chosen, kinetics[s], kinetic)
            source_target = jnp.where(chosen, targets[s], source_target)
        source_targets.append(source_target)
        factors.append(kinetic)
        for row in range(9):
            pieces_of[row].append([rows[9 * g + row : 9 * g + row + 1] for g in range(whole)])
            if width % PAIR:
                at = 9 * whole + row % 4 if row < 8 else 9 * whole + 4
                tail = rows[at : at + 1, NA:] if 4 <= row < 8 else rows[at : at + 1, :NA]
                pieces_of[row][-1].append(tail)
    mean = jnp.concatenate(factors, axis=0) / (3.0 * atoms) + motion_work_lower_limit
    source_target = jnp.concatenate(source_targets, axis=0)
    target = jnp.concatenate(targets, axis=0)
    factor = jnp.sqrt(source_target / mean) * jnp.sqrt(target / source_target)
    for row in range(9):
        for index in range(len(pieces_of[row][0])):
            value = jnp.concatenate([of_replica[index] for of_replica in pieces_of[row]], axis=0)
            size = value.shape[1]
            if row // 3 == 1:
                value = value * factor[:, :size]
            outs[row // 3][row % 3, :, index * PAIR : index * PAIR + size] = value


def run_prepare(state, features, per_replica, weights, small):
    atoms, channels = features.shape
    own_pairs = atoms // per_replica // PAIR
    extended = own_pairs + 2
    return pl.pallas_call(
        functools.partial(prepare, per_replica),
        out_shape=(
            jax.ShapeDtypeStruct((extended, 8, PAIR), jnp.float32),
            jax.ShapeDtypeStruct((own_pairs, 8, PAIR), jnp.float32),
            jax.ShapeDtypeStruct((extended * PAIR, channels), jnp.bfloat16),
            jax.ShapeDtypeStruct((extended * PAIR, channels), jnp.bfloat16),
            jax.ShapeDtypeStruct(((extended - 1) * PAIR, channels), jnp.float32),
            jax.ShapeDtypeStruct((8, channels), jnp.float32),
        ),
        in_specs=[VMEM_SPEC] * 4,
        out_specs=(VMEM_SPEC,) * 6,
        compiler_params=pltpu.CompilerParams(vmem_limit_bytes=20 * 1024 * 1024),
    )(state, features, weights, small)


def advance_last(stage, parts_count, *refs):
    inputs, last, state, rest = refs[:STEP_INPUTS], refs[STEP_INPUTS], refs[STEP_INPUTS + 1 :][:3], refs[STEP_INPUTS + 4 :]
    advance(stage, parts_count, *inputs, *state, last, *rest)


def run_advance(stage, parts_count, last_shape, x, v, g, edge, got, own_feat, table, message_push, later_push, weights, small):
    own_pairs = v.shape[0]
    channels = table.shape[1]
    basis_count = small.shape[0] - SMALL_ROWS
    tiles = jax.ShapeDtypeStruct(v.shape, jnp.float32)
    lhs = pltpu.VMEM(((basis_count + 3) * NA, PAIR), jnp.bfloat16)
    vec = pltpu.VMEM((3 * NA, PAIR), jnp.bfloat16)
    message = pltpu.VMEM((PAIR, 2 * channels), jnp.bfloat16)
    last = stage == 3
    state = [] if last else [tiles] * 3
    outs = pl.pallas_call(
        functools.partial(advance_last if last else advance, stage, parts_count),
        out_shape=(*state, jax.ShapeDtypeStruct(last_shape, jnp.float32)),
        in_specs=[VMEM_SPEC] * STEP_INPUTS,
        out_specs=(VMEM_SPEC,) * (len(state) + 1),
        scratch_shapes=([pltpu.VMEM(v.shape, jnp.float32)] * 3 if last else [])
        + [
            pltpu.VMEM((own_pairs + 2, 8, PAIR), jnp.float32),
            pltpu.VMEM((own_pairs + 1, 8, PAIR), jnp.float32),
            [[lhs] * 3] * 2,
            [[vec] * 3] * 2,
            message,
            message,
            pltpu.VMEM((own_pairs + 2, 3, 8, PAIR), jnp.float32),
        ],
        compiler_params=pltpu.CompilerParams(vmem_limit_bytes=20 * 1024 * 1024),
    )(x, v, g, edge, got, own_feat, table, message_push, later_push, weights, small)
    return (None, None, None, *outs) if last else outs


def run_steps(state, features, per_replica, chunk_shape, exchange, weights, small):
    x, v, *fixed = run_prepare(state, features, per_replica, weights, small)
    edge_shape = (2, 2, 8, PAIR)
    edge = got = jnp.zeros(edge_shape, jnp.float32)
    g = v
    for step in range(STEPS + 1):
        stage = min(step, 2) if step < STEPS else 3
        shape = edge_shape if step < STEPS else chunk_shape
        x, v, g, edge = run_advance(stage, per_replica, shape, x, v, g, edge, got, *fixed, weights, small)
        if step < STEPS:
            got = exchange(edge)
    return edge


def run_finish(ladder, got, local_atoms):
    replicas = ladder.shape[1]
    out = jax.ShapeDtypeStruct((3, replicas, local_atoms), jnp.float32)
    whole = pl.BlockSpec(out.shape, lambda: (0, 0, 0))
    outs = pl.pallas_call(
        finish,
        out_shape=(out, out, out),
        in_specs=[VMEM_SPEC] * 2,
        out_specs=(whole, whole, whole),
        compiler_params=pltpu.CompilerParams(vmem_limit_bytes=8 * 1024 * 1024),
    )(ladder, got)
    return tuple(jnp.transpose(o, (1, 0, 2)) for o in outs)


def on_device(
    particle_places,
    particle_speeds,
    thermal_targets,
    element_features,
    swap_counterpart_slot,
    swap_approval_flags,
    initial_signal_projector,
    initial_distance_filter,
    initial_directional_scales,
    invariant_revision_matrix,
    magnitude_revision_matrix,
    later_signal_projector,
    later_directional_scales,
    push_output_matrix,
):
    replicas = particle_places.shape[0]
    local_atoms = particle_places.shape[2]
    local_cells = local_atoms // NA
    devices = lax.axis_size("dom")
    own = lax.axis_index("dom")
    per_replica = devices // replicas
    bits = devices.bit_length() - 1
    replica_bits = replicas.bit_length() - 1

    def trade(value, mask):
        return lax.ppermute(value, "dom", [(i, i ^ mask) for i in range(devices)])

    weights = jnp.concatenate(
        [initial_signal_projector, invariant_revision_matrix, magnitude_revision_matrix, later_signal_projector], axis=0
    )
    span = initial_distance_filter.shape[0] - 1
    order = (jnp.arange(span + 1, dtype=jnp.float32) - 0.5 * span)[:, None]
    channels = element_features.shape[1]
    part = own % per_replica
    cells = float(devices * local_cells)
    thermal = lax.dynamic_slice(thermal_targets, (own // per_replica,), (1,))
    small = jnp.concatenate(
        [
            initial_distance_filter * jnp.exp(-2.0 * order * order),
            (initial_directional_scales * initial_directional_scales)[None],
            (push_output_matrix * initial_directional_scales)[None],
            (push_output_matrix * later_directional_scales)[None],
            jnp.broadcast_to(thermal[:, None], (1, channels)),
            jnp.broadcast_to(jnp.where(part == 0, -cells, 0.0), (1, channels)),
            jnp.broadcast_to(jnp.where(part == per_replica - 1, cells, 0.0), (1, channels)),
            jnp.broadcast_to(part.astype(jnp.float32), (1, channels)),
        ],
        axis=0,
    )

    slots = jnp.arange(replicas, dtype=jnp.int32)
    source = jnp.where(swap_approval_flags > 0, swap_counterpart_slot, slots)
    ladder = jnp.stack([thermal_targets, source.astype(jnp.float32)])

    atom_cell = jnp.arange(local_atoms, dtype=jnp.int32) // NA
    cell_floor = jnp.array([0.0, 0.0, 1.0], jnp.float32)[:, None] * (
        own * local_cells + atom_cell
    ).astype(jnp.float32)
    state = jnp.concatenate([particle_places - cell_floor, particle_speeds], axis=1)
    upper_part = lax.reduce_precision(state, 8, 7)
    state = jnp.stack([upper_part, state - upper_part], axis=1).astype(jnp.bfloat16)
    channels = element_features.shape[1]
    state = state.reshape(replicas, -1, channels)
    state_rows = state.shape[1]
    features = element_features
    for level in range(bits):
        mask = devices >> (level + 1)
        upper = (own & mask) > 0
        if level < replica_bits:
            half = state.shape[0] // 2
            keep = jnp.where(upper, state[half:], state[:half])
            send = jnp.where(upper, state[:half], state[half:])
        else:
            keep = send = state
        message = jnp.concatenate([features.reshape(-1, channels), send.reshape(-1, channels)], axis=0)
        if level == 1:
            message, weights, small, ladder = lax.optimization_barrier((message, weights, small, ladder))
        got = trade(message, mask)
        count = features.size // channels
        got_features = got[:count].reshape(features.shape)
        got = got[count:].reshape(send.shape)
        axis = 1 + level
        state = jnp.stack([jnp.where(upper, got, keep), jnp.where(upper, keep, got)], axis=axis)
        features = jnp.stack(
            [jnp.where(upper, got_features, features), jnp.where(upper, features, got_features)], axis=level
        )
    state = state.reshape(devices, 2, 6, local_atoms).astype(jnp.float32)
    state = (state[:, 0] + state[:, 1]).transpose(1, 0, 2).reshape(6, devices * local_atoms)
    features = features.reshape(devices * local_atoms, -1)

    def exchange(edge):
        if per_replica == 2:
            return trade(edge, 1)
        groups = [list(range(i, i + per_replica)) for i in range(0, devices, per_replica)]
        up = [(a, b) for g in groups for a, b in zip(g, g[1:] + g[:1])]
        kinetic = lax.psum(edge[0, 1, 3], "dom", axis_index_groups=groups) - edge[0, 1, 3]
        before = lax.ppermute(edge[1], "dom", up)
        after = lax.ppermute(edge[0], "dom", [(b, a) for a, b in up])
        return jnp.stack([after.at[1, 3].set(kinetic), before])

    chunk_rows = 9 * (local_atoms // PAIR) + (5 if local_atoms % PAIR else 0) + 1
    chunk_rows = -(-chunk_rows // 8) * 8
    chunks = run_steps(state, features, per_replica, (devices, chunk_rows, PAIR), exchange, weights, small)
    got = lax.all_to_all(chunks.astype(jnp.bfloat16), "dom", 0, 0)
    return run_finish(ladder, got, local_atoms)


def solution(mesh):
    return jax.shard_map(
        on_device,
        mesh=mesh,
        in_specs=(
            P("groups", None, "dom"),
            P("groups", None, "dom"),
            P("groups"),
            P(("groups", "dom"), None),
            P("groups"),
            P("groups"),
            P(),
            P(),
            P(),
            P(),
            P(),
            P(),
            P(),
            P(),
        ),
        out_specs=(P("groups", None, "dom"), P("groups", None, "dom"), P("groups", None, "dom")),
        check_vma=False,
    )
```
